128 devices in a mesh: head: 8 (over y_lo, x), vocab: 16 (over y_hi, z, core).
Axes of the slice: x: 4, y: 4 (y_hi: 2, y_lo: 2; y = y_hi * 2 + y_lo), z: 4, core: 2. Of those that a mesh axis runs over, the one named last changes fastest.
Arguments:
- hidden_rows: bfloat16 [512, 2048], P(('head', 'vocab')), may hold values from -240 to 240
- head_weight: bfloat16 [8, 2048, 32768], P('head', None, 'vocab'), may hold values from -0.125 to 0.125
- teacher_logits: bfloat16 [8, 512, 32768], P('head', 'vocab'), may hold values from -24 to 336
Outputs:
- weight_grad: bfloat16 [8, 2048, 32768], P('head', None, 'vocab')
- input_grad: float32 [512, 2048], P(('head', 'vocab'))
The draws below stay inside these ranges and needn't reach their ends.
All inputs are finite; a program needn't handle non-finite values.
Results may differ from the reference program's by a relative error of at most 0.004.
Values may be sent and summed in bfloat16 or wider, within the bound.
A program may use at most 128 MiB of HBM per device.

```python
import jax
import jax.numpy as jnp
from jax import lax

D = 2048
TOK = 512
VOCAB = 32768
HEADS = 8


def draw_hidden_rows(key, part):
    first_key, second_key = jax.random.split(key)
    values = jnp.clip(jax.random.normal(first_key, (TOK, D), jnp.float32), -6.0, 6.0)
    scales = jnp.exp(jax.random.uniform(second_key, (TOK, 1), jnp.float32, jnp.log(3.0), jnp.log(30.0)))
    return (values * scales).astype(jnp.bfloat16)


def draw_teacher_logits(key, part):
    first_key = jax.random.fold_in(key, 0)
    values = 3.0 * jnp.clip(jax.random.normal(first_key, (HEADS, TOK, VOCAB), jnp.float32), -8.0, 8.0)
    return values.astype(jnp.bfloat16)


def steps_of(stream_key, dims, cuts, least, high):
    factor_of = 1.0
    for axis_at, parts in cuts:
        steps = jax.random.uniform(jax.random.fold_in(jax.random.fold_in(stream_key, 6), axis_at), (parts,), jnp.float32, least / len(cuts), high / len(cuts))
        factor_of = factor_of * jnp.repeat(jnp.exp(steps), dims[axis_at] // parts).reshape((-1,) + (1,) * (len(dims) - 1 - axis_at))
    return factor_of


def gaussian(rng, shape, spread, limit, cuts=(), dtype=jnp.bfloat16):
    gain = steps_of(rng, shape, cuts, -0.22, 0.18) if cuts else 1.0
    result = jax.random.normal(rng, shape, jnp.float32) * spread * gain
    return jnp.minimum(jnp.maximum(result, -limit), limit).astype(dtype)


def setup_inputs(seed: int = 0) -> dict:
    key_of = jax.random.split(jax.random.key(seed), 4)
    hidden_rows = draw_hidden_rows(jax.random.fold_in(key_of[3], 71), 0)
    head_weight = gaussian(key_of[1], (HEADS, D, VOCAB), D ** -0.5, 0.125, ((0, 8), (2, 16)))
    teacher_logits = draw_teacher_logits(jax.random.fold_in(key_of[3], 71), 0)
    return dict(hidden_rows=hidden_rows, head_weight=head_weight, teacher_logits=teacher_logits)


def reference(hidden_rows, head_weight, teacher_logits):
    def per_head(pair):
        weight, teacher = pair
        student = jnp.dot(hidden_rows, weight, preferred_element_type=jnp.float32)
        student_prob = jax.nn.softmax(student, axis=1)
        teacher_prob = jax.nn.softmax(teacher.astype(jnp.float32), axis=1)
        logit_grad = (student_prob - teacher_prob).astype(jnp.bfloat16)
        weight_grad = jnp.dot(hidden_rows.T, logit_grad, preferred_element_type=jnp.float32).astype(jnp.bfloat16)
        grad_part = jnp.dot(logit_grad, weight.T, preferred_element_type=jnp.float32)
        return weight_grad, grad_part

    weight_grad, grad_parts = lax.map(per_head, (head_weight, teacher_logits))
    return weight_grad, jnp.sum(grad_parts, axis=0)
```

```python
import jax
import jax.numpy as jnp
from jax import lax
from jax.experimental import pallas as pl
from jax.experimental.pallas import tpu as pltpu
from jax.sharding import PartitionSpec as P

MESH = pl.DeviceIdType.MESH
F32, BF16 = jnp.float32, jnp.bfloat16
HEAD, VOC, CHIPS = 8, 16, 8
D, TOK, COLS = 2048, 512, 2048
ROWS = TOK // VOC
HR = TOK // HEAD
HALF = D // 2
CW = 256
NC = COLS // CW
DK = HALF // CW


def kernel(
    h_ref, w_hbm, t_hbm, wg_hbm, out_ref,
    w_v, t_v, tbuf, h32, st1, hs, hb, ht, e_v, te_v, lg_v, wg_v,
    col, tst_src, tstat, stx, sbuf, x0s, x0r, r1s, r1r, r2s, r2r, r3s, r3r,
    local_sem, wg_sem,
    s1, r1, sa, ra, stt, rtt, s2, r2, sf, rf, sst, rst, sx, rx, sr1, rr1, sr2, rr2, sr3, rr3,
):
    hd, vc = lax.axis_index("head"), lax.axis_index("vocab")
    chip = vc // 2
    core = vc - 2 * chip
    sib = 2 * chip + 1 - core

    def rows_of(index, count):
        return pl.ds(pl.multiple_of(index * count, count), count)

    def each(start, stop, body):
        def step(j, carry):
            body(j)
            return carry
        lax.fori_loop(start, stop, step, 0)

    def voc(j):
        return lax.rem(vc + j, VOC)

    def voc_from(j):
        return lax.rem(vc + VOC - j, VOC)

    def head(j):
        return lax.rem(hd + j, HEAD)

    def head_from(j):
        return lax.rem(hd + HEAD - j, HEAD)

    def remote(src, dst, send, recv, **to):
        return pltpu.make_async_remote_copy(
            src_ref=src, dst_ref=dst, send_sem=send, recv_sem=recv, device_id=to, device_id_type=MESH
        )

    w_copy = pltpu.make_async_copy(w_hbm, w_v, local_sem.at[0])
    t_copy = pltpu.make_async_copy(t_hbm, t_v, local_sem.at[1])
    own_tile = pltpu.make_async_copy(
        t_hbm.at[:, rows_of(vc, COLS)], tbuf.at[rows_of(vc, ROWS), :], local_sem.at[2]
    )
    t_copy.start()
    w_copy.start()
    own_tile.start()
    h32[0] = h_ref[:, :HALF].astype(F32)
    h32[1] = h_ref[:, HALF:].astype(F32)

    barrier = pltpu.get_barrier_semaphore()
    each(1, VOC, lambda j: pl.semaphore_signal(barrier, inc=1, device_id={"vocab": voc(j)}, device_id_type=MESH))
    each(1, HEAD, lambda j: pl.semaphore_signal(barrier, inc=1, device_id={"head": head(j)}, device_id_type=MESH))
    pl.semaphore_wait(barrier, VOC - 1 + HEAD - 1)

    def ag1(j, owner, to):
        return remote(h32.at[lax.rem(to, 2)], st1.at[owner], s1.at[j], r1.at[j], vocab=to)

    each(1, VOC, lambda j: ag1(j, vc, voc(j)).start())

    def a2a(j, owner, to):
        return remote(
            t_hbm.at[:, rows_of(to, COLS)], tbuf.at[rows_of(owner, ROWS), :], sa.at[j], ra.at[j], vocab=to
        )

    each(1, VOC, lambda j: a2a(j, vc, voc(j)).start())

    st1[vc] = h32[core]
    each(1, VOC, lambda j: ag1(j, voc_from(j), voc(j)).wait_recv())
    for i in range(VOC):
        hs[4 * i : 4 * i + 4, :] = st1[i]
    hb[core, rows_of(hd, HR), :] = hs[...].astype(BF16)

    def ag2(j, owner):
        block = hb.at[core, rows_of(owner, HR), :]
        return remote(block, block, s2.at[j], r2.at[j], head=head(j))

    def fwd(j, owner, side):
        block = hb.at[side, rows_of(owner, HR), :]
        return remote(block, block, sf.at[j], rf.at[j], vocab=sib)

    each(1, HEAD, lambda j: ag2(j, hd).start())
    fwd(0, hd, core).start()

    t_copy.wait()
    TW = 2048

    def top_step(i, top):
        x = t_v[:, pl.ds(pl.multiple_of(i * TW, TW), TW)].astype(F32)
        for k in range(TW // 128):
            top = jnp.maximum(top, x[:, k * 128 : (k + 1) * 128])
        return top

    top = lax.fori_loop(0, COLS * VOC // TW, top_step, jnp.full((ROWS, 128), -jnp.inf, F32))
    top = jnp.broadcast_to(jnp.max(top, axis=1, keepdims=True), (ROWS, 128))

    def sum_step(i, total):
        x = t_v[:, pl.ds(pl.multiple_of(i * TW, TW), TW)].astype(F32)
        for k in range(TW // 128):
            total = total + jnp.exp(x[:, k * 128 : (k + 1) * 128] - top)
        return total

    total = lax.fori_loop(0, COLS * VOC // TW, sum_step, jnp.zeros((ROWS, 128), F32))
    scale = 1.0 / jnp.broadcast_to(jnp.sum(total, axis=1, keepdims=True), (ROWS, 128))
    lane = lax.broadcasted_iota(jnp.int32, (ROWS, 128), 1)
    both = jnp.where(lane < 64, top, scale)
    tst_src[...] = both
    tstat[rows_of(vc, ROWS), :] = both

    def tst(j, owner):
        return remote(tst_src, tstat.at[rows_of(owner, ROWS), :], stt.at[j], rtt.at[j], vocab=voc(j))

    each(1, VOC, lambda j: tst(j, vc).start())

    def pass_on(j):
        ag2(j, head_from(j)).wait_recv()
        fwd(j, head_from(j), core).start()

    each(1, HEAD, pass_on)
    fwd(0, hd, 1 - core).wait_recv()
    each(1, HEAD, lambda j: fwd(j, head_from(j), 1 - core).wait_recv())
    w_copy.wait()

    col[0] = jnp.full((TOK, 128), -jnp.inf, F32)

    def student_step(n):
        cols = pl.ds(pl.multiple_of(n * CW, CW), CW)
        x = jnp.dot(hb[0], w_v[:HALF, cols], preferred_element_type=F32)
        x = x + jnp.dot(hb[1], w_v[HALF:, cols], preferred_element_type=F32)
        e_v[n] = x
        col[0] = jnp.maximum(col[0], jnp.maximum(x[:, :128], x[:, 128:]))

    each(0, NC, student_step)
    col[0] = jnp.broadcast_to(jnp.max(col[0], axis=1, keepdims=True), (TOK, 128))
    col[1] = jnp.zeros((TOK, 128), F32)

    def exp_step(n):
        top_n = col[0]
        a = jnp.exp(e_v[n, :, :128] - top_n)
        b = jnp.exp(e_v[n, :, 128:] - top_n)
        e_v[n, :, :128] = a
        e_v[n, :, 128:] = b
        col[1] = col[1] + (a + b)

    each(0, NC, exp_step)
    sums = jnp.broadcast_to(jnp.sum(col[1], axis=1, keepdims=True), (TOK, 128))
    lane_t = lax.broadcasted_iota(jnp.int32, (TOK, 128), 1)
    stats = jnp.where(lane_t == 0, col[0], sums).T[:8, :]
    stx[...] = stats
    sbuf[vc] = stats

    def st(j, owner):
        return remote(stx, sbuf.at[owner], sst.at[j], rst.at[j], vocab=voc(j))

    each(1, VOC, lambda j: st(j, vc).start())

    for half in range(2):
        for k in range(DK):
            ht[half * HALF + k * CW : half * HALF + (k + 1) * CW, :] = hb[half, :, k * CW : (k + 1) * CW].T

    own_tile.wait()
    each(1, VOC, lambda j: tst(j, voc_from(j)).wait_recv())
    each(1, VOC, lambda j: a2a(j, voc_from(j), voc(j)).wait_recv())
    col[0] = jnp.broadcast_to(tstat[:, 0:1], (TOK, 128))
    col[1] = jnp.broadcast_to(tstat[:, 64:65], (TOK, 128))

    def teacher_step(n):
        for side in range(2):
            cols = pl.ds(pl.multiple_of(n * CW + side * 128, 128), 128)
            x = tbuf[:, cols].astype(F32)
            te_v[n, :, side * 128 : side * 128 + 128] = jnp.exp(x - col[0]) * col[1]

    each(0, NC, teacher_step)

    each(1, VOC, lambda j: st(j, voc_from(j)).wait_recv())
    tops = [sbuf[i][0:1, :] for i in range(VOC)]
    parts = [sbuf[i][1:2, :] for i in range(VOC)]
    top_all = tops[0]
    for x in tops[1:]:
        top_all = jnp.maximum(top_all, x)
    total_all = jnp.zeros_like(top_all)
    for x, y in zip(tops, parts):
        total_all = total_all + y * jnp.exp(x - top_all)
    factor = jnp.exp(stx[0:1, :] - top_all) / total_all
    col[0] = jnp.broadcast_to(factor, (128, TOK)).T

    def grad_step(n):
        for side in range(2):
            cols = pl.ds(pl.multiple_of(n * CW + side * 128, 128), 128)
            lanes = slice(side * 128, side * 128 + 128)
            lg_v[:, cols] = (e_v[n, :, lanes] * col[0] - te_v[n, :, lanes]).astype(BF16)

    each(0, NC, grad_step)

    def share(half, k):
        rows = pl.ds(pl.multiple_of(half * HALF + k * CW, CW), CW)
        return lax.dot_general(
            lg_v[...], w_v[rows, :], (((1,), (1,)), ((), ())), preferred_element_type=F32
        )

    def x0(k):
        return remote(x0s.at[k], x0r.at[k], sx.at[k], rx.at[k], vocab=sib)

    def give_step(k):
        x0s[k] = share(1 - core, k).astype(BF16)
        x0(k).start()

    each(0, DK, give_step)

    def rs1(k, j, to, owner):
        return remote(
            r1s.at[k, to], r1r.at[k, owner], sr1.at[k * HEAD + j], rr1.at[k * HEAD + j], head=head(j)
        )

    def keep_step(k):
        mine = share(core, k)
        x0(k).wait_recv()
        r1s[k] = (mine + x0r[k].astype(F32)).astype(BF16).reshape(HEAD, HR, CW)
        each(1, HEAD, lambda j: rs1(k, j, head(j), hd).start())
        r1r[k, hd] = r1s[k, hd]

    each(0, DK, keep_step)

    def wg_out(n):
        rows = pl.ds(pl.multiple_of(n * CW, CW), CW)
        return pltpu.make_async_copy(wg_v.at[rows, :], wg_hbm.at[rows, :], wg_sem.at[n])

    def weight_step(n):
        rows = pl.ds(pl.multiple_of(n * CW, CW), CW)
        wg_v[rows, :] = jnp.dot(ht[rows, :], lg_v[...], preferred_element_type=F32).astype(BF16)
        wg_out(n).start()

    each(0, D // CW, weight_step)

    for k in range(DK):
        each(1, HEAD, lambda j: rs1(k, j, head(j), head_from(j)).wait_recv())
        total = r1r[k, 0].astype(F32)
        for i in range(1, HEAD):
            total = total + r1r[k, i].astype(F32)
        r2s[:, :, k * CW : (k + 1) * CW] = total.reshape(CHIPS, 8, CW)

    def rs2(j, to, owner):
        return remote(r2s.at[to], r2r.at[owner], sr2.at[j], rr2.at[j], vocab=2 * to + core)

    def chip_at(j):
        return lax.rem(chip + j, CHIPS)

    each(1, CHIPS, lambda j: rs2(j, chip_at(j), chip).start())
    r2r[chip] = r2s[chip]
    each(1, CHIPS, lambda j: rs2(j, chip_at(j), lax.rem(chip + CHIPS - j, CHIPS)).wait_recv())
    mine = r2r[0]
    for i in range(1, CHIPS):
        mine = mine + r2r[i]
    r3s[...] = mine
    rs3 = remote(r3s, r3r, sr3, rr3, vocab=sib)
    rs3.start()
    rs3.wait_recv()
    other = r3r[...]
    first = core == 0
    low = jnp.where(first, mine, other)
    high = jnp.where(first, other, mine)
    out_ref[:, :HALF] = jnp.where(first, low[:4], low[4:])
    out_ref[:, HALF:] = jnp.where(first, high[:4], high[4:])

    each(1, VOC, lambda j: ag1(j, vc, voc(j)).wait_send())
    each(1, VOC, lambda j: a2a(j, vc, voc(j)).wait_send())
    each(1, VOC, lambda j: tst(j, vc).wait_send())
    each(1, VOC, lambda j: st(j, vc).wait_send())
    each(1, HEAD, lambda j: ag2(j, hd).wait_send())
    each(0, HEAD, lambda j: fwd(j, head_from(j), core).wait_send())
    each(0, DK, lambda k: x0(k).wait_send())
    for k in range(DK):
        each(1, HEAD, lambda j: rs1(k, j, head(j), hd).wait_send())
    each(1, CHIPS, lambda j: rs2(j, chip_at(j), chip).wait_send())
    rs3.wait_send()
    each(0, D // CW, lambda n: wg_out(n).wait())


def per_device(hidden_rows, head_weight, teacher_logits):
    hbm = pl.BlockSpec(memory_space=pltpu.MemorySpace.HBM)
    vmem = pl.BlockSpec(memory_space=pltpu.VMEM)
    dma = pltpu.SemaphoreType.DMA
    weight_grad, input_grad = pl.pallas_call(
        kernel,
        out_shape=(
            jax.ShapeDtypeStruct((D, COLS), BF16),
            jax.ShapeDtypeStruct((TOK // (HEAD * VOC), D), F32),
        ),
        in_specs=[vmem, hbm, hbm],
        out_specs=(hbm, vmem),
        scratch_shapes=[
            pltpu.VMEM((D, COLS), BF16),
            pltpu.VMEM((ROWS, COLS * VOC), BF16),
            pltpu.VMEM((TOK, COLS), BF16),
            pltpu.VMEM((2, 4, HALF), F32),
            pltpu.VMEM((VOC, 4, HALF), F32),
            pltpu.VMEM((HR, HALF), F32),
            pltpu.VMEM((2, TOK, HALF), BF16),
            pltpu.VMEM((D, TOK), BF16),
            pltpu.VMEM((NC, TOK, CW), F32),
            pltpu.VMEM((NC, TOK, CW), F32),
            pltpu.VMEM((TOK, COLS), BF16),
            pltpu.VMEM((D, COLS), BF16),
            pltpu.VMEM((2, TOK, 128), F32),
            pltpu.VMEM((ROWS, 128), F32),
            pltpu.VMEM((TOK, 128), F32),
            pltpu.VMEM((8, TOK), F32),
            pltpu.VMEM((VOC, 8, TOK), F32),
            pltpu.VMEM((DK, TOK, CW), BF16),
            pltpu.VMEM((DK, TOK, CW), BF16),
            pltpu.VMEM((DK, HEAD, HR, CW), BF16),
            pltpu.VMEM((DK, HEAD, HR, CW), BF16),
            pltpu.VMEM((CHIPS, 8, HALF), F32),
            pltpu.VMEM((CHIPS, 8, HALF), F32),
            pltpu.VMEM((8, HALF), F32),
            pltpu.VMEM((8, HALF), F32),
            dma((3,)), dma((D // CW,)),
            dma((VOC,)), dma((VOC,)), dma((VOC,)), dma((VOC,)), dma((VOC,)), dma((VOC,)),
            dma((HEAD,)), dma((HEAD,)), dma((HEAD,)), dma((HEAD,)),
            dma((VOC,)), dma((VOC,)), dma((DK,)), dma((DK,)),
            dma((DK * HEAD,)), dma((DK * HEAD,)), dma((CHIPS,)), dma((CHIPS,)), dma, dma,
        ],
        compiler_params=pltpu.CompilerParams(
            collective_id=0, has_side_effects=True, vmem_limit_bytes=56 * 1024 * 1024
        ),
        cost_estimate=pl.CostEstimate(
            flops=6 * TOK * D * COLS, bytes_accessed=20 * 1024 * 1024, transcendentals=3 * TOK * COLS
        ),
    )(hidden_rows, head_weight[0], teacher_logits[0])
    return weight_grad[None], input_grad


def solution(mesh):
    return jax.shard_map(
        per_device,
        mesh=mesh,
        in_specs=(P(("head", "vocab"), None), P("head", None, "vocab"), P("head", "vocab", None)),
        out_specs=(P("head", None, "vocab"), P(("head", "vocab"), None)),
        check_vma=False,
    )
```

```python
import jax
import jax.numpy as jnp
from jax import lax
from jax.experimental import pallas as pl
from jax.experimental.pallas import tpu as pltpu
from jax.sharding import PartitionSpec as P

MESH = pl.DeviceIdType.MESH
F32, BF16 = jnp.float32, jnp.bfloat16
HEAD, VOC, CHIPS = 8, 16, 8
D, TOK, COLS = 2048, 512, 2048
ROWS = TOK // VOC
HR = TOK // HEAD
HALF = D // 2
CW = 256
NC = COLS // CW
DK = HALF // CW


def kernel(
    h_ref, w_hbm, t_hbm, wg_v, out_ref,
    w_v, t_v, tbuf, pack, own, st1, hs, hb, ht, e_v, lg_v,
    col, tst_src, tstat, stx, sbuf, x0s, x0r, r1s, r1r, r2s, r2r, r3s, r3r,
    local_sem,
    s1, r1, sa, ra, stt, rtt, s2, r2, sf, rf, sst, rst, sx, rx, sr1, rr1, sr2, rr2, sr3, rr3,
):
    hd, vc = lax.axis_index("head"), lax.axis_index("vocab")
    chip = vc // 2
    core = vc - 2 * chip
    sib = 2 * chip + 1 - core

    def rows_of(index, count):
        return pl.ds(pl.multiple_of(index * count, count), count)

    def each(start, stop, body):
        def step(j, carry):
            body(j)
            return carry
        lax.fori_loop(start, stop, step, 0)

    def voc(j):
        return lax.rem(vc + j, VOC)

    def voc_from(j):
        return lax.rem(vc + VOC - j, VOC)

    def head(j):
        return lax.rem(hd + j, HEAD)

    def head_from(j):
        return lax.rem(hd + HEAD - j, HEAD)

    def remote(src, dst, send, recv, **to):
        return pltpu.make_async_remote_copy(
            src_ref=src, dst_ref=dst, send_sem=send, recv_sem=recv, device_id=to, device_id_type=MESH
        )

    w_copy = pltpu.make_async_copy(w_hbm, w_v, local_sem.at[0])
    t_copy = pltpu.make_async_copy(t_hbm, t_v, local_sem.at[1])
    own_tile = pltpu.make_async_copy(
        t_hbm.at[:, rows_of(vc, COLS)], tbuf.at[rows_of(vc, ROWS), :], local_sem.at[2]
    )
    t_copy.start()
    w_copy.start()
    own_tile.start()
    for side in range(2):
        for g in range(4):
            at = side * HALF + g * CW
            pack[4 * g : 4 * g + 4, :] = h_ref[:, at : at + CW].astype(F32)
        own[side] = pack[...].astype(BF16)

    barrier = pltpu.get_barrier_semaphore()
    each(1, VOC, lambda j: pl.semaphore_signal(barrier, inc=1, device_id={"vocab": voc(j)}, device_id_type=MESH))
    each(1, HEAD, lambda j: pl.semaphore_signal(barrier, inc=1, device_id={"head": head(j)}, device_id_type=MESH))
    pl.semaphore_wait(barrier, VOC - 1 + HEAD - 1)

    def ag1(j, owner, to):
        return remote(own.at[lax.rem(to, 2)], st1.at[owner], s1.at[j], r1.at[j], vocab=to)

    each(1, VOC, lambda j: ag1(j, vc, voc(j)).start())

    y_hi = vc // 8

    def tile_to(j):
        near = lax.rem(vc + j, 8)
        return 8 * lax.rem(y_hi + j // 8, 2) + near

    def tile_from(j):
        near = lax.rem(vc + 16 - j, 8)
        return 8 * lax.rem(y_hi + j // 8, 2) + near

    def a2a(j, owner, to):
        return remote(
            t_hbm.at[:, rows_of(to, COLS)], tbuf.at[rows_of(owner, ROWS), :], sa.at[j], ra.at[j], vocab=to
        )

    each(1, 8, lambda j: a2a(j, vc, tile_to(j)).start())

    st1[vc] = own[core]
    each(1, VOC, lambda j: ag1(j, voc_from(j), voc(j)).wait_recv())
    for i in range(VOC):
        rows = st1[i].astype(F32)
        for g in range(4):
            hs[4 * i : 4 * i + 4, g * CW : (g + 1) * CW] = rows[4 * g : 4 * g + 4, :]
    hb[core, rows_of(hd, HR), :] = hs[...].astype(BF16)

    y_lo = hd // 4
    x_at = hd - 4 * y_lo

    def head_at(p, j):
        return 4 * lax.rem(y_lo + p, 2) + lax.rem(x_at + 4 + j, 4)

    def block(side, p, j):
        return hb.at[side, rows_of(head_at(p, j), HR), :]

    def agy(p):
        return remote(block(core, p, 0), block(core, p, 0), s2.at[0], r2.at[0], head=head_at(1, 0))

    def agx(p, j, src):
        return remote(
            block(core, p, src), block(core, p, src), s2.at[4 * p + j], r2.at[4 * p + j], head=head_at(0, j)
        )

    def fwd(p, j, side):
        at = block(side, p, -j)
        return remote(at, at, sf.at[4 * p + j], rf.at[4 * p + j], vocab=sib)

    agy(0).start()
    each(1, 4, lambda j: agx(0, j, 0).start())
    fwd(0, 0, core).start()
    each(8, VOC, lambda j: a2a(j, vc, tile_to(j)).start())
    agy(1).wait_recv()
    each(1, 4, lambda j: agx(1, j, 0).start())
    fwd(1, 0, core).start()

    t_copy.wait()
    TW = 2048

    def top_step(i, top):
        x = t_v[:, pl.ds(pl.multiple_of(i * TW, TW), TW)].astype(F32)
        for k in range(TW // 128):
            top = jnp.maximum(top, x[:, k * 128 : (k + 1) * 128])
        return top

    top = lax.fori_loop(0, COLS * VOC // TW, top_step, jnp.full((ROWS, 128), -jnp.inf, F32))
    top = jnp.broadcast_to(jnp.max(top, axis=1, keepdims=True), (ROWS, 128))

    def sum_step(i, total):
        x = t_v[:, pl.ds(pl.multiple_of(i * TW, TW), TW)].astype(F32)
        for k in range(TW // 128):
            total = total + jnp.exp(x[:, k * 128 : (k + 1) * 128] - top)
        return total

    total = lax.fori_loop(0, COLS * VOC // TW, sum_step, jnp.zeros((ROWS, 128), F32))
    scale = 1.0 / jnp.broadcast_to(jnp.sum(total, axis=1, keepdims=True), (ROWS, 128))
    lane = lax.broadcasted_iota(jnp.int32, (ROWS, 128), 1)
    both = jnp.concatenate([jnp.where(lane == 0, top, scale), jnp.zeros((128 - ROWS, 128), F32)])
    tst_src[...] = both.T[:8]
    tstat[vc] = tst_src[...]

    def tst(j, owner):
        return remote(tst_src, tstat.at[owner], stt.at[j], rtt.at[j], vocab=voc(j))

    each(1, VOC, lambda j: tst(j, vc).start())

    for p in range(2):
        def pass_on(j):
            agx(p, j, -j).wait_recv()
            fwd(p, j, core).start()

        each(1, 4, pass_on)
    for p in range(2):
        each(0, 4, lambda j: fwd(p, j, 1 - core).wait_recv())
    w_copy.wait()

    col[0] = jnp.full((TOK, 128), -jnp.inf, F32)

    def student_step(n):
        cols = pl.ds(pl.multiple_of(n * CW, CW), CW)
        x = jnp.dot(hb[0], w_v[:HALF, cols], preferred_element_type=F32)
        x = x + jnp.dot(hb[1], w_v[HALF:, cols], preferred_element_type=F32)
        e_v[n] = x
        col[0] = jnp.maximum(col[0], jnp.maximum(x[:, :128], x[:, 128:]))

    each(0, NC, student_step)
    col[0] = jnp.broadcast_to(jnp.max(col[0], axis=1, keepdims=True), (TOK, 128))
    col[1] = jnp.zeros((TOK, 128), F32)

    def exp_step(n):
        top_n = col[0]
        a = jnp.exp(e_v[n, :, :128] - top_n)
        b = jnp.exp(e_v[n, :, 128:] - top_n)
        e_v[n, :, :128] = a
        e_v[n, :, 128:] = b
        col[1] = col[1] + (a + b)

    each(0, NC, exp_step)
    sums = jnp.broadcast_to(jnp.sum(col[1], axis=1, keepdims=True), (TOK, 128))
    lane_t = lax.broadcasted_iota(jnp.int32, (TOK, 128), 1)
    stats = jnp.where(lane_t == 0, col[0], sums).T[:8, :]
    for i in range(4):
        stx[i : i + 1, :] = stats[0:1, i * 128 : (i + 1) * 128]
        stx[4 + i : 5 + i, :] = stats[1:2, i * 128 : (i + 1) * 128]
    sbuf[vc] = stx[...]

    def st(j, owner):
        return remote(stx, sbuf.at[owner], sst.at[j], rst.at[j], vocab=voc(j))

    each(1, VOC, lambda j: st(j, vc).start())

    for half in range(2):
        for k in range(DK):
            ht[half * HALF + k * CW : half * HALF + (k + 1) * CW, :] = hb[half, :, k * CW : (k + 1) * CW].T

    each(1, VOC, lambda j: tst(j, voc_from(j)).wait_recv())
    for i in range(4):
        rows = jnp.concatenate([tstat[4 * i + k][:, :ROWS] for k in range(4)], axis=1)
        rows = jnp.concatenate([rows, jnp.zeros((120, 128), F32)]).T
        col[0, i * 128 : (i + 1) * 128, :] = jnp.broadcast_to(rows[:, 0:1], (128, 128))
        col[1, i * 128 : (i + 1) * 128, :] = jnp.broadcast_to(rows[:, 1:2], (128, 128))

    each(1, VOC, lambda j: st(j, voc_from(j)).wait_recv())
    tops = [sbuf[i][:4] for i in range(VOC)]
    parts = [sbuf[i][4:] for i in range(VOC)]
    top_all = tops[0]
    for x in tops[1:]:
        top_all = jnp.maximum(top_all, x)
    total_all = jnp.zeros_like(top_all)
    for x, y in zip(tops, parts):
        total_all = total_all + y * jnp.exp(x - top_all)
    factor = jnp.exp(stx[:4] - top_all) / total_all
    for i in range(4):
        col[2, i * 128 : (i + 1) * 128, :] = jnp.broadcast_to(factor[i : i + 1], (128, 128)).T

    own_tile.wait()
    each(1, VOC, lambda j: a2a(j, tile_from(j), tile_to(j)).wait_recv())

    def grad_step(n):
        for side in range(2):
            cols = pl.ds(pl.multiple_of(n * CW + side * 128, 128), 128)
            teacher = jnp.exp(tbuf[:, cols].astype(F32) - col[0]) * col[1]
            student = e_v[n, :, side * 128 : side * 128 + 128] * col[2]
            lg_v[:, cols] = (student - teacher).astype(BF16)

    each(0, NC, grad_step)

    def share(half, k):
        rows = pl.ds(pl.multiple_of(half * HALF + k * CW, CW), CW)
        return lax.dot_general(
            lg_v[...], w_v[rows, :], (((1,), (1,)), ((), ())), preferred_element_type=F32
        )

    def x0(k):
        return remote(x0s.at[k], x0r.at[k], sx.at[k], rx.at[k], vocab=sib)

    def give_step(k):
        x0s[k] = share(1 - core, k).astype(BF16)
        x0(k).start()

    each(0, DK, give_step)

    def rs1(k, j, to, owner):
        return remote(
            r1s.at[k, to], r1r.at[k, owner], sr1.at[k * HEAD + j], rr1.at[k * HEAD + j], head=head(j)
        )

    def keep_step(k):
        mine = share(core, k)
        x0(k).wait_recv()
        r1s[k] = (mine + x0r[k].astype(F32)).astype(BF16).reshape(HEAD, HR, CW)
        each(1, HEAD, lambda j: rs1(k, j, head(j), hd).start())
        r1r[k, hd] = r1s[k, hd]

    each(0, DK, keep_step)

    def weight_step(n):
        rows = pl.ds(pl.multiple_of(n * CW, CW), CW)
        wg_v[rows, :] = jnp.dot(ht[rows, :], lg_v[...], preferred_element_type=F32).astype(BF16)

    each(0, D // CW, weight_step)

    for k in range(DK):
        each(1, HEAD, lambda j: rs1(k, j, head(j), head_from(j)).wait_recv())
        total = r1r[k, 0].astype(F32)
        for i in range(1, HEAD):
            total = total + r1r[k, i].astype(F32)
        r2s[:, :, k * CW : (k + 1) * CW] = total.reshape(CHIPS, 8, CW)

    def rs2(j, to, owner):
        return remote(r2s.at[to], r2r.at[owner], sr2.at[j], rr2.at[j], vocab=2 * to + core)

    def chip_at(j):
        return lax.rem(chip + j, CHIPS)

    each(1, CHIPS, lambda j: rs2(j, chip_at(j), chip).start())
    r2r[chip] = r2s[chip]
    each(1, CHIPS, lambda j: rs2(j, chip_at(j), lax.rem(chip + CHIPS - j, CHIPS)).wait_recv())
    mine = r2r[0]
    for i in range(1, CHIPS):
        mine = mine + r2r[i]
    r3s[...] = mine
    rs3 = remote(r3s, r3r, sr3, rr3, vocab=sib)
    rs3.start()
    rs3.wait_recv()
    other = r3r[...]
    first = core == 0
    low = jnp.where(first, mine, other)
    high = jnp.where(first, other, mine)
    out_ref[:, :HALF] = jnp.where(first, low[:4], low[4:])
    out_ref[:, HALF:] = jnp.where(first, high[:4], high[4:])

    each(1, VOC, lambda j: ag1(j, vc, voc(j)).wait_send())
    each(1, VOC, lambda j: a2a(j, vc, tile_to(j)).wait_send())
    each(1, VOC, lambda j: tst(j, vc).wait_send())
    each(1, VOC, lambda j: st(j, vc).wait_send())
    agy(0).wait_send()
    for p in range(2):
        each(1, 4, lambda j: agx(p, j, 0).wait_send())
        each(0, 4, lambda j: fwd(p, j, core).wait_send())
    each(0, DK, lambda k: x0(k).wait_send())
    for k in range(DK):
        each(1, HEAD, lambda j: rs1(k, j, head(j), hd).wait_send())
    each(1, CHIPS, lambda j: rs2(j, chip_at(j), chip).wait_send())
    rs3.wait_send()


def per_device(hidden_rows, head_weight, teacher_logits):
    hbm = pl.BlockSpec(memory_space=pltpu.MemorySpace.HBM)
    vmem = pl.BlockSpec(memory_space=pltpu.VMEM)
    dma = pltpu.SemaphoreType.DMA
    weight_grad, input_grad = pl.pallas_call(
        kernel,
        out_shape=(
            pltpu.VMEM((D, COLS), BF16),
            jax.ShapeDtypeStruct((TOK // (HEAD * VOC), D), F32),
        ),
        in_specs=[vmem, hbm, hbm],
        out_specs=(vmem, vmem),
        scratch_shapes=[
            pltpu.VMEM((D, COLS), BF16),
            pltpu.VMEM((ROWS, COLS * VOC), BF16),
            pltpu.VMEM((TOK, COLS), BF16),
            pltpu.VMEM((16, CW), F32),
            pltpu.VMEM((2, 16, CW), BF16),
            pltpu.VMEM((VOC, 16, CW), BF16),
            pltpu.VMEM((HR, HALF), F32),
            pltpu.VMEM((2, TOK, HALF), BF16),
            pltpu.VMEM((D, TOK), BF16),
            pltpu.VMEM((NC, TOK, CW), F32),
            pltpu.VMEM((TOK, COLS), BF16),
            pltpu.VMEM((3, TOK, 128), F32),
            pltpu.VMEM((8, 128), F32),
            pltpu.VMEM((VOC, 8, 128), F32),
            pltpu.VMEM((8, 128), F32),
            pltpu.VMEM((VOC, 8, 128), F32),
            pltpu.VMEM((DK, TOK, CW), BF16),
            pltpu.VMEM((DK, TOK, CW), BF16),
            pltpu.VMEM((DK, HEAD, HR, CW), BF16),
            pltpu.VMEM((DK, HEAD, HR, CW), BF16),
            pltpu.VMEM((CHIPS, 8, HALF), F32),
            pltpu.VMEM((CHIPS, 8, HALF), F32),
            pltpu.VMEM((8, HALF), F32),
            pltpu.VMEM((8, HALF), F32),
            dma((3,)),
            dma((VOC,)), dma((VOC,)), dma((VOC,)), dma((VOC,)), dma((VOC,)), dma((VOC,)),
            dma((HEAD,)), dma((HEAD,)), dma((HEAD,)), dma((HEAD,)),
            dma((VOC,)), dma((VOC,)), dma((DK,)), dma((DK,)),
            dma((DK * HEAD,)), dma((DK * HEAD,)), dma((CHIPS,)), dma((CHIPS,)), dma, dma,
        ],
        compiler_params=pltpu.CompilerParams(
            collective_id=0, has_side_effects=True, vmem_limit_bytes=44 * 1024 * 1024
        ),
        cost_estimate=pl.CostEstimate(
            flops=6 * TOK * D * COLS, bytes_accessed=20 * 1024 * 1024, transcendentals=3 * TOK * COLS
        ),
    )(hidden_rows, head_weight[0], teacher_logits[0])
    return weight_grad[None], input_grad


def solution(mesh):
    return jax.shard_map(
        per_device,
        mesh=mesh,
        in_specs=(P(("head", "vocab"), None), P("head", None, "vocab"), P("head", "vocab", None)),
        out_specs=(P("head", None, "vocab"), P(("head", "vocab"), None)),
        check_vma=False,
    )
```

```python
import jax
import jax.numpy as jnp
from jax import lax
from jax.experimental import pallas as pl
from jax.experimental.pallas import tpu as pltpu
from jax.sharding import PartitionSpec as P

MESH = pl.DeviceIdType.MESH
F32, BF16 = jnp.float32, jnp.bfloat16
HEAD, VOC, CHIPS = 8, 16, 8
D, TOK, COLS = 2048, 512, 2048
ROWS = TOK // VOC
HR = TOK // HEAD
HALF = D // 2
CW = 256
NC = COLS // CW
DK = HALF // CW


def kernel(
    h_ref, w_hbm, t_hbm, wg_v, out_ref,
    w_v, t_v, tbuf, pack, own, st1, hs, hb, ht, e_v, lg_v,
    col, tst_src, tstat, stx, sbuf, x0s, x0r,
    a1s, a1r, a2s, a2r, a3s, a3r, b1s, b1r, b2s, b2r, r3s, r3r,
    local_sem,
    s1, r1, sa, ra, stt, rtt, s2, r2, sf, rf, sst, rst, sx, rx,
    sa1, ra1, sa2, ra2, sa3, ra3, sb1, rb1, sb2, rb2, sr3, rr3,
):
    hd, vc = lax.axis_index("head"), lax.axis_index("vocab")
    chip = vc // 2
    core = vc - 2 * chip
    sib = 2 * chip + 1 - core

    def rows_of(index, count):
        return pl.ds(pl.multiple_of(index * count, count), count)

    def each(start, stop, body):
        def step(j, carry):
            body(j)
            return carry
        lax.fori_loop(start, stop, step, 0)

    def voc(j):
        return lax.rem(vc + j, VOC)

    def voc_from(j):
        return lax.rem(vc + VOC - j, VOC)

    y_hi, y_lo = vc // 8, hd // 4
    x_at = hd - 4 * y_lo

    def head_at(p, j):
        return 4 * lax.rem(y_lo + p, 2) + lax.rem(x_at + 4 + j, 4)

    def remote(src, dst, send, recv, **to):
        return pltpu.make_async_remote_copy(
            src_ref=src, dst_ref=dst, send_sem=send, recv_sem=recv, device_id=to, device_id_type=MESH
        )

    w_copy = pltpu.make_async_copy(w_hbm, w_v, local_sem.at[0])
    t_copy = pltpu.make_async_copy(t_hbm, t_v, local_sem.at[1])
    own_tile = pltpu.make_async_copy(
        t_hbm.at[:, rows_of(vc, COLS)], tbuf.at[rows_of(vc, ROWS), :], local_sem.at[2]
    )
    t_copy.start()
    w_copy.start()
    own_tile.start()
    for side in range(2):
        for g in range(4):
            at = side * HALF + g * CW
            pack[4 * g : 4 * g + 4, :] = h_ref[:, at : at + CW].astype(F32)
        own[side] = pack[...].astype(BF16)

    barrier = pltpu.get_barrier_semaphore()

    def greet(**to):
        pl.semaphore_signal(barrier, inc=1, device_id=to, device_id_type=MESH)

    each(1, VOC, lambda j: greet(vocab=voc(j)))
    each(0, VOC, lambda j: greet(head=head_at(1, 0), vocab=voc(j)))
    for p in range(2):
        each(1, 4, lambda j: greet(head=head_at(p, j)))
    pl.semaphore_wait(barrier, 2 * VOC - 1 + 6)

    def ag1(p, j, owner, to):
        return remote(
            own.at[lax.rem(to, 2)], st1.at[VOC * p + owner], s1.at[VOC * p + j], r1.at[VOC * p + j],
            head=head_at(p, 0), vocab=to,
        )

    each(1, VOC, lambda j: ag1(0, j, vc, voc(j)).start())
    each(0, VOC, lambda j: ag1(1, j, vc, voc(j)).start())

    def tile_to(j):
        return 8 * lax.rem(y_hi + j // 8, 2) + lax.rem(vc + j, 8)

    def tile_from(j):
        return 8 * lax.rem(y_hi + j // 8, 2) + lax.rem(vc + 16 - j, 8)

    def a2a(j, owner, to):
        return remote(
            t_hbm.at[:, rows_of(to, COLS)], tbuf.at[rows_of(owner, ROWS), :], sa.at[j], ra.at[j], vocab=to
        )

    each(8, VOC, lambda j: a2a(j, vc, tile_to(j)).start())
    each(1, 8, lambda j: a2a(j, vc, tile_to(j)).start())

    def block(side, p, j):
        return hb.at[side, rows_of(head_at(p, j), HR), :]

    def agx(p, j, src):
        return remote(
            block(core, p, src), block(core, p, src), s2.at[4 * p + j], r2.at[4 * p + j], head=head_at(0, j)
        )

    def fwd(p, j, side):
        at = block(side, p, -j)
        return remote(at, at, sf.at[4 * p + j], rf.at[4 * p + j], vocab=sib)

    st1[vc] = own[core]
    for p in range(2):
        each(1 - p, VOC, lambda j: ag1(p, j, voc_from(j), voc(j)).wait_recv())
        for i in range(VOC):
            rows = st1[VOC * p + i].astype(F32)
            for g in range(4):
                hs[4 * i : 4 * i + 4, g * CW : (g + 1) * CW] = rows[4 * g : 4 * g + 4, :]
        hb[core, rows_of(head_at(p, 0), HR), :] = hs[...].astype(BF16)
        agx(p, 1, 0).start()
        agx(p, 3, 0).start()
        fwd(p, 0, core).start()
    for p in range(2):
        agx(p, 2, 0).start()

    t_copy.wait()
    TW = 2048

    def top_step(i, top):
        x = t_v[:, pl.ds(pl.multiple_of(i * TW, TW), TW)].astype(F32)
        for k in range(TW // 128):
            top = jnp.maximum(top, x[:, k * 128 : (k + 1) * 128])
        return top

    top = lax.fori_loop(0, COLS * VOC // TW, top_step, jnp.full((ROWS, 128), -jnp.inf, F32))
    top = jnp.broadcast_to(jnp.max(top, axis=1, keepdims=True), (ROWS, 128))

    def sum_step(i, total):
        x = t_v[:, pl.ds(pl.multiple_of(i * TW, TW), TW)].astype(F32)
        for k in range(TW // 128):
            total = total + jnp.exp(x[:, k * 128 : (k + 1) * 128] - top)
        return total

    total = lax.fori_loop(0, COLS * VOC // TW, sum_step, jnp.zeros((ROWS, 128), F32))
    scale = 1.0 / jnp.broadcast_to(jnp.sum(total, axis=1, keepdims=True), (ROWS, 128))
    lane = lax.broadcasted_iota(jnp.int32, (ROWS, 128), 1)
    both = jnp.concatenate([jnp.where(lane == 0, top, scale), jnp.zeros((128 - ROWS, 128), F32)])
    tst_src[...] = both.T[:8]
    tstat[vc] = tst_src[...]

    def tst(j, owner):
        return remote(tst_src, tstat.at[owner], stt.at[j], rtt.at[j], vocab=voc(j))

    each(1, VOC, lambda j: tst(j, vc).start())

    def student(places):
        places = [(p, j) for j in places for p in range(2)]
        for p, j in places:
            if j:
                agx(p, j, -j).wait_recv()
                fwd(p, j, core).start()
        for p, j in places:
            fwd(p, j, 1 - core).wait_recv()
        blocks = [rows_of(head_at(p, -j), HR) for p, j in places]
        if 0 in [j for _, j in places]:
            w_copy.wait()
        for rows in blocks:
            col[0, rows, :] = jnp.full((HR, 128), -jnp.inf, F32)
            col[1, rows, :] = jnp.zeros((HR, 128), F32)

        def logit_step(n):
            cols = pl.ds(pl.multiple_of(n * CW, CW), CW)
            low = jnp.concatenate([hb[0, rows, :] for rows in blocks])
            x = jnp.dot(low, w_v[:HALF, cols], preferred_element_type=F32)
            high = jnp.concatenate([hb[1, rows, :] for rows in blocks])
            x = x + jnp.dot(high, w_v[HALF:, cols], preferred_element_type=F32)
            for i, rows in enumerate(blocks):
                part = x[i * HR : (i + 1) * HR]
                e_v[n, rows, :] = part
                col[0, rows, :] = jnp.maximum(col[0, rows, :], jnp.maximum(part[:, :128], part[:, 128:]))

        each(0, NC, logit_step)
        for rows in blocks:
            col[0, rows, :] = jnp.broadcast_to(jnp.max(col[0, rows, :], axis=1, keepdims=True), (HR, 128))

        def exp_step(n):
            for rows in blocks:
                a = jnp.exp(e_v[n, rows, :128] - col[0, rows, :])
                b = jnp.exp(e_v[n, rows, 128:] - col[0, rows, :])
                e_v[n, rows, :128] = a
                e_v[n, rows, 128:] = b
                col[1, rows, :] = col[1, rows, :] + (a + b)

        each(0, NC, exp_step)

    student((0, 1, 3))
    student((2,))
    sums = jnp.broadcast_to(jnp.sum(col[1], axis=1, keepdims=True), (TOK, 128))
    lane_t = lax.broadcasted_iota(jnp.int32, (TOK, 128), 1)
    stats = jnp.where(lane_t == 0, col[0], sums).T[:8, :]
    for i in range(4):
        stx[i : i + 1, :] = stats[0:1, i * 128 : (i + 1) * 128]
        stx[4 + i : 5 + i, :] = stats[1:2, i * 128 : (i + 1) * 128]
    sbuf[vc] = stx[...]

    def st(j, owner):
        return remote(stx, sbuf.at[owner], sst.at[j], rst.at[j], vocab=voc(j))

    each(1, VOC, lambda j: st(j, vc).start())

    for half in range(2):
        for k in range(DK):
            ht[half * HALF + k * CW : half * HALF + (k + 1) * CW, :] = hb[half, :, k * CW : (k + 1) * CW].T

    each(1, VOC, lambda j: tst(j, voc_from(j)).wait_recv())
    for i in range(4):
        rows = jnp.concatenate([tstat[4 * i + k][:, :ROWS] for k in range(4)], axis=1)
        rows = jnp.concatenate([rows, jnp.zeros((120, 128), F32)]).T
        col[0, i * 128 : (i + 1) * 128, :] = jnp.broadcast_to(rows[:, 0:1], (128, 128))
        col[1, i * 128 : (i + 1) * 128, :] = jnp.broadcast_to(rows[:, 1:2], (128, 128))

    each(1, VOC, lambda j: st(j, voc_from(j)).wait_recv())
    tops = [sbuf[i][:4] for i in range(VOC)]
    parts = [sbuf[i][4:] for i in range(VOC)]
    top_all = tops[0]
    for x in tops[1:]:
        top_all = jnp.maximum(top_all, x)
    total_all = jnp.zeros_like(top_all)
    for x, y in zip(tops, parts):
        total_all = total_all + y * jnp.exp(x - top_all)
    factor = jnp.exp(stx[:4] - top_all) / total_all
    for i in range(4):
        col[2, i * 128 : (i + 1) * 128, :] = jnp.broadcast_to(factor[i : i + 1], (128, 128)).T

    own_tile.wait()
    each(1, VOC, lambda j: a2a(j, tile_from(j), tile_to(j)).wait_recv())

    def grad_step(n):
        for side in range(2):
            cols = pl.ds(pl.multiple_of(n * CW + side * 128, 128), 128)
            teacher = jnp.exp(tbuf[:, cols].astype(F32) - col[0]) * col[1]
            student = e_v[n, :, side * 128 : side * 128 + 128] * col[2]
            lg_v[:, cols] = (student - teacher).astype(BF16)

    each(0, NC, grad_step)

    def share(half, k):
        rows = pl.ds(pl.multiple_of(half * HALF + k * CW, CW), CW)
        return lax.dot_general(
            lg_v[...], w_v[rows, :], (((1,), (1,)), ((), ())), preferred_element_type=F32
        )

    def x0(k):
        return remote(x0s.at[k], x0r.at[k], sx.at[k], rx.at[k], vocab=sib)

    def give(k):
        x0s[k] = share(1 - core, k).astype(BF16)
        x0(k).start()

    def both_cores(k):
        mine = share(core, k)
        x0(k).wait_recv()
        return mine + x0r[k].astype(F32)

    def chip_at(j):
        return lax.rem(chip + CHIPS + j, CHIPS)

    def a1(k, j):
        return remote(
            a1s.at[k, lax.rem(x_at + j, 4)], a1r.at[k, x_at], sa1.at[4 * k + j], ra1.at[4 * k + j], head=head_at(0, j)
        )

    def keep_a(k):
        mine = both_cores(k)
        for y in range(2):
            for x in range(4):
                at = (4 * y + x) * HR
                a1s[k, x, y] = mine[at : at + HR].astype(BF16)
        for j in (1, 3, 2):
            a1(k, j).start()
        a1r[k, x_at] = a1s[k, x_at]

    def a2(k):
        return remote(a2s.at[k, lax.rem(y_lo + 1, 2)], a2r.at[k], sa2.at[k], ra2.at[k], head=head_at(1, 0))

    def a3(j):
        return remote(a3s.at[chip_at(j)], a3r.at[chip], sa3.at[j], ra3.at[j], vocab=2 * chip_at(j) + core)

    def b1(k, j):
        return remote(
            b1s.at[k, chip_at(j)], b1r.at[k, chip], sb1.at[8 * k + j], rb1.at[8 * k + j], vocab=2 * chip_at(j) + core
        )

    def keep_b(k):
        mine = both_cores(2 + k).reshape(HEAD, CHIPS, 8, CW)
        for q in range(CHIPS):
            b1s[k, q] = mine[:, q].reshape(HEAD * 8, CW).astype(BF16)
        each(1, CHIPS, lambda j: b1(k, j).start())
        b1r[k, chip] = b1s[k, chip]

    def b2(j):
        to = lax.rem(hd + j, HEAD)
        return remote(b2s.at[to], b2r.at[hd], sb2.at[j], rb2.at[j], head=to)

    give(0)
    give(1)
    keep_a(0)
    give(2)
    keep_a(1)
    give(3)
    keep_b(0)
    keep_b(1)

    def weight_step(n):
        rows = pl.ds(pl.multiple_of(n * CW, CW), CW)
        wg_v[rows, :] = jnp.dot(ht[rows, :], lg_v[...], preferred_element_type=F32).astype(BF16)

    def total_of(ref, k, count):
        total = ref[k, 0].astype(F32)
        for i in range(1, count):
            total = total + ref[k, i].astype(F32)
        return total

    for k in range(2):
        for j in (1, 3, 2):
            a1(k, j).wait_recv()
        a2s[k] = total_of(a1r, k, 4)
        a2(k).start()

    each(0, NC // 2, weight_step)

    for k in range(2):
        each(1, CHIPS, lambda j: b1(k, j).wait_recv())
        b2s[:, :, k * CW : (k + 1) * CW] = total_of(b1r, k, CHIPS).reshape(HEAD, 8, CW)
    each(1, HEAD, lambda j: b2(j).start())
    b2r[hd] = b2s[hd]
    for k in range(2):
        a2(k).wait_recv()
        a3s[:, :, k * CW : (k + 1) * CW] = (a2s[k, y_lo] + a2r[k]).reshape(CHIPS, 8, CW)
    each(1, CHIPS, lambda j: a3(j).start())
    a3r[chip] = a3s[chip]

    each(NC // 2, NC, weight_step)

    def sum_of(ref):
        total = ref[0]
        for i in range(1, 8):
            total = total + ref[i]
        return total

    each(1, HEAD, lambda j: b2(j).wait_recv())
    r3s[:, HALF // 2 :] = sum_of(b2r)
    each(1, CHIPS, lambda j: a3(j).wait_recv())
    r3s[:, : HALF // 2] = sum_of(a3r)
    mine = r3s[...]
    rs3 = remote(r3s, r3r, sr3, rr3, vocab=sib)
    rs3.start()
    rs3.wait_recv()
    other = r3r[...]
    first = core == 0
    low = jnp.where(first, mine, other)
    high = jnp.where(first, other, mine)
    out_ref[:, :HALF] = jnp.where(first, low[:4], low[4:])
    out_ref[:, HALF:] = jnp.where(first, high[:4], high[4:])

    for p in range(2):
        each(1 - p, VOC, lambda j: ag1(p, j, vc, voc(j)).wait_send())
    each(1, VOC, lambda j: a2a(j, vc, tile_to(j)).wait_send())
    each(1, VOC, lambda j: tst(j, vc).wait_send())
    each(1, VOC, lambda j: st(j, vc).wait_send())
    for p in range(2):
        each(1, 4, lambda j: agx(p, j, 0).wait_send())
        each(0, 4, lambda j: fwd(p, j, core).wait_send())
    each(0, DK, lambda k: x0(k).wait_send())
    for k in range(2):
        for j in range(1, 4):
            a1(k, j).wait_send()
        a2(k).wait_send()
        each(1, CHIPS, lambda j: b1(k, j).wait_send())
    each(1, CHIPS, lambda j: a3(j).wait_send())
    each(1, HEAD, lambda j: b2(j).wait_send())
    rs3.wait_send()


def per_device(hidden_rows, head_weight, teacher_logits):
    hbm = pl.BlockSpec(memory_space=pltpu.MemorySpace.HBM)
    vmem = pl.BlockSpec(memory_space=pltpu.VMEM)
    dma = pltpu.SemaphoreType.DMA
    weight_grad, input_grad = pl.pallas_call(
        kernel,
        out_shape=(
            pltpu.VMEM((D, COLS), BF16),
            jax.ShapeDtypeStruct((TOK // (HEAD * VOC), D), F32),
        ),
        in_specs=[vmem, hbm, hbm],
        out_specs=(vmem, vmem),
        scratch_shapes=[
            pltpu.VMEM((D, COLS), BF16),
            pltpu.VMEM((ROWS, COLS * VOC), BF16),
            pltpu.VMEM((TOK, COLS), BF16),
            pltpu.VMEM((16, CW), F32),
            pltpu.VMEM((2, 16, CW), BF16),
            pltpu.VMEM((2 * VOC, 16, CW), BF16),
            pltpu.VMEM((HR, HALF), F32),
            pltpu.VMEM((2, TOK, HALF), BF16),
            pltpu.VMEM((D, TOK), BF16),
            pltpu.VMEM((NC, TOK, CW), F32),
            pltpu.VMEM((TOK, COLS), BF16),
            pltpu.VMEM((3, TOK, 128), F32),
            pltpu.VMEM((8, 128), F32),
            pltpu.VMEM((VOC, 8, 128), F32),
            pltpu.VMEM((8, 128), F32),
            pltpu.VMEM((VOC, 8, 128), F32),
            pltpu.VMEM((DK, TOK, CW), BF16),
            pltpu.VMEM((DK, TOK, CW), BF16),
            pltpu.VMEM((2, 4, 2, HR, CW), BF16),
            pltpu.VMEM((2, 4, 2, HR, CW), BF16),
            pltpu.VMEM((2, 2, HR, CW), F32),
            pltpu.VMEM((2, HR, CW), F32),
            pltpu.VMEM((CHIPS, 8, HALF // 2), F32),
            pltpu.VMEM((CHIPS, 8, HALF // 2), F32),
            pltpu.VMEM((2, CHIPS, HEAD * 8, CW), BF16),
            pltpu.VMEM((2, CHIPS, HEAD * 8, CW), BF16),
            pltpu.VMEM((HEAD, 8, HALF // 2), F32),
            pltpu.VMEM((HEAD, 8, HALF // 2), F32),
            pltpu.VMEM((8, HALF), F32),
            pltpu.VMEM((8, HALF), F32),
            dma((3,)),
            dma((2 * VOC,)), dma((2 * VOC,)), dma((VOC,)), dma((VOC,)), dma((VOC,)), dma((VOC,)),
            dma((HEAD,)), dma((HEAD,)), dma((HEAD,)), dma((HEAD,)), dma((VOC,)), dma((VOC,)), dma((DK,)), dma((DK,)),
            dma((8,)), dma((8,)), dma((2,)), dma((2,)), dma((CHIPS,)), dma((CHIPS,)),
            dma((2 * CHIPS,)), dma((2 * CHIPS,)), dma((HEAD,)), dma((HEAD,)), dma, dma,
        ],
        compiler_params=pltpu.CompilerParams(
            collective_id=0, has_side_effects=True, vmem_limit_bytes=44 * 1024 * 1024
        ),
        cost_estimate=pl.CostEstimate(
            flops=6 * TOK * D * COLS, bytes_accessed=20 * 1024 * 1024, transcendentals=3 * TOK * COLS
        ),
    )(hidden_rows, head_weight[0], teacher_logits[0])
    return weight_grad[None], input_grad


def solution(mesh):
    return jax.shard_map(
        per_device,
        mesh=mesh,
        in_specs=(P(("head", "vocab"), None), P("head", None, "vocab"), P("head", "vocab", None)),
        out_specs=(P("head", None, "vocab"), P(("head", "vocab"), None)),
        check_vma=False,
    )
```

```python
import jax
import jax.numpy as jnp
from jax import lax
from jax.experimental import pallas as pl
from jax.experimental.pallas import tpu as pltpu
from jax.sharding import PartitionSpec as P

MESH = pl.DeviceIdType.MESH
F32, BF16 = jnp.float32, jnp.bfloat16
HEAD, VOC, CHIPS = 8, 16, 8
D, TOK, COLS = 2048, 512, 2048
ROWS = TOK // VOC
HR = TOK // HEAD
HALF = D // 2
CW = 256
NC = COLS // CW
BW = 512
NB = COLS // BW
GR = TOK // 2
WG_FIRST = 3
DK = HALF // BW


def kernel(
    h_ref, w_hbm, t_hbm, wg_v, out_ref,
    w_v, t_v, tbuf, pack, own, st1, hs, hb, ht, e_v, lg_v,
    col, tcol, tst_src, tstat, stx, sbuf, x0s, x0r,
    a1s, a1r, a2s, a2r, b1s, b1r, b2s, b2r, r3s, r3r,
    local_sem,
    s1, r1, sa, ra, stt, rtt, s2, r2, sf, rf, sst, rst, sx, rx,
    sa1, ra1, sa2, ra2, sb1, rb1, sb2, rb2, sr3, rr3,
):
    hd, vc = lax.axis_index("head"), lax.axis_index("vocab")
    chip = vc // 2
    core = vc - 2 * chip
    sib = 2 * chip + 1 - core

    def rows_of(index, count):
        return pl.ds(pl.multiple_of(index * count, count), count)

    def each(start, stop, body):
        def step(j, carry):
            body(j)
            return carry
        lax.fori_loop(start, stop, step, 0)

    def voc(j):
        return lax.rem(vc + j, VOC)

    def voc_from(j):
        return lax.rem(vc + VOC - j, VOC)

    y_hi, y_lo = vc // 8, hd // 4
    x_at = hd - 4 * y_lo

    def y_of(group):
        return lax.rem(y_hi + group, 2)

    def head_at(group, j):
        return 4 * y_of(group) + lax.rem(x_at + 4 + j, 4)

    def beside(p):
        return 4 * lax.rem(y_lo + p, 2) + x_at

    def along_x(j):
        return 4 * y_lo + lax.rem(x_at + j, 4)

    def remote(src, dst, send, recv, **to):
        return pltpu.make_async_remote_copy(
            src_ref=src, dst_ref=dst, send_sem=send, recv_sem=recv, device_id=to, device_id_type=MESH
        )

    w_copy = pltpu.make_async_copy(w_hbm, w_v, local_sem.at[0])
    t_copy = pltpu.make_async_copy(t_hbm, t_v, local_sem.at[1])
    own_tile = pltpu.make_async_copy(
        t_hbm.at[:, rows_of(vc, COLS)], tbuf.at[rows_of(vc, ROWS), :], local_sem.at[2]
    )
    t_copy.start()
    w_copy.start()
    own_tile.start()
    for side in range(2):
        for g in range(4):
            at = side * HALF + g * CW
            pack[4 * g : 4 * g + 4, :] = h_ref[:, at : at + CW].astype(F32)
        own[side] = pack[...].astype(BF16)

    barrier = pltpu.get_barrier_semaphore()

    def greet(**to):
        pl.semaphore_signal(barrier, inc=1, device_id=to, device_id_type=MESH)

    each(1, VOC, lambda j: greet(vocab=voc(j)))
    each(0, VOC, lambda j: greet(head=beside(1), vocab=voc(j)))
    each(1, 4, lambda j: greet(head=along_x(j)))
    each(1, 4, lambda j: greet(head=4 * lax.rem(y_lo + 1, 2) + lax.rem(x_at + j, 4)))
    pl.semaphore_wait(barrier, 2 * VOC - 1 + 6)

    def ag1(p, j, owner, to):
        return remote(
            own.at[lax.rem(to, 2)], st1.at[owner], s1.at[VOC * p + j], r1.at[VOC * p + j],
            head=beside(p), vocab=to,
        )

    each(1, VOC, lambda j: ag1(0, j, VOC * y_lo + vc, voc(j)).start())
    each(0, VOC, lambda j: ag1(1, j, VOC * y_lo + vc, voc(j)).start())

    def tile_to(j):
        return 8 * lax.rem(y_hi + j // 8, 2) + lax.rem(vc + j, 8)

    def tile_from(j):
        return 8 * lax.rem(y_hi + j // 8, 2) + lax.rem(vc + 16 - j, 8)

    def a2a(j, owner, to):
        return remote(
            t_hbm.at[:, rows_of(to, COLS)], tbuf.at[rows_of(owner, ROWS), :], sa.at[j], ra.at[j], vocab=to
        )

    each(8, VOC, lambda j: a2a(j, vc, tile_to(j)).start())
    each(1, 8, lambda j: a2a(j, vc, tile_to(j)).start())

    def block(side, p, j):
        return hb.at[side, rows_of(head_at(p, j), HR), :]

    def agx(p, j, src):
        return remote(
            block(core, p, src), block(core, p, src), s2.at[4 * p + j], r2.at[4 * p + j], head=along_x(j)
        )

    def fwd(p, j, side):
        at = block(side, p, -j)
        return remote(at, at, sf.at[4 * p + j], rf.at[4 * p + j], vocab=sib)

    t_copy.wait()
    TW = 2048

    def top_step(i, top):
        x = t_v[:, pl.ds(pl.multiple_of(i * TW, TW), TW)].astype(F32)
        for k in range(TW // 128):
            top = jnp.maximum(top, x[:, k * 128 : (k + 1) * 128])
        return top

    top = lax.fori_loop(0, COLS * VOC // TW, top_step, jnp.full((ROWS, 128), -jnp.inf, F32))
    top = jnp.broadcast_to(jnp.max(top, axis=1, keepdims=True), (ROWS, 128))

    def sum_step(i, total):
        x = t_v[:, pl.ds(pl.multiple_of(i * TW, TW), TW)].astype(F32)
        for k in range(TW // 128):
            total = total + jnp.exp(x[:, k * 128 : (k + 1) * 128] - top)
        return total

    total = lax.fori_loop(0, COLS * VOC // TW, sum_step, jnp.zeros((ROWS, 128), F32))
    scale = 1.0 / jnp.broadcast_to(jnp.sum(total, axis=1, keepdims=True), (ROWS, 128))
    lane = lax.broadcasted_iota(jnp.int32, (ROWS, 128), 1)
    both = jnp.concatenate([jnp.where(lane == 0, top, scale), jnp.zeros((128 - ROWS, 128), F32)])
    tst_src[...] = both.T[:8]
    tstat[vc] = tst_src[...]

    def tst(j, owner):
        return remote(tst_src, tstat.at[owner], stt.at[j], rtt.at[j], vocab=voc(j))

    each(1, VOC, lambda j: tst(j, vc).start())

    st1[VOC * y_lo + vc] = own[core]
    for p in range(2):
        each(1 - p, VOC, lambda j: ag1(p, j, VOC * lax.rem(y_lo + p, 2) + voc_from(j), voc(j)).wait_recv())
    for group in range(2):
        for i in range(VOC):
            rows = st1[VOC * y_of(group) + i].astype(F32)
            for g in range(4):
                hs[4 * i : 4 * i + 4, g * CW : (g + 1) * CW] = rows[4 * g : 4 * g + 4, :]
        hb[core, rows_of(head_at(group, 0), HR), :] = hs[...].astype(BF16)
        if group == 0:
            for j in (1, 3, 2):
                agx(0, j, 0).start()
        fwd(group, 0, core).start()

    def group_rows(group):
        return rows_of(y_of(group), GR)

    def st(group, j, owner):
        at = VOC * y_of(group) + j
        return remote(stx.at[group], sbuf.at[y_of(group), owner], sst.at[at], rst.at[at], vocab=voc(j))

    def student(group):
        rows = group_rows(group)
        if group == 0:
            each(1, 4, lambda j: agx(0, j, 0).wait_send())
            for j in (1, 3, 2):
                agx(1, j, 0).start()
        for j in (1, 3, 2):
            agx(group, j, -j).wait_recv()
            fwd(group, j, core).start()
        each(0, 4, lambda j: fwd(group, j, 1 - core).wait_recv())
        if group == 0:
            w_copy.wait()
        col[0] = jnp.full((GR, 128), -jnp.inf, F32)
        col[1] = jnp.zeros((GR, 128), F32)

        def logit_step(n):
            cols = pl.ds(pl.multiple_of(n * BW, BW), BW)
            x = jnp.dot(hb[0, rows, :], w_v[:HALF, cols], preferred_element_type=F32)
            x = x + jnp.dot(hb[1, rows, :], w_v[HALF:, cols], preferred_element_type=F32)
            e_v[n, rows, :] = x
            top_n = col[0]
            for i in range(BW // 128):
                top_n = jnp.maximum(top_n, x[:, i * 128 : (i + 1) * 128])
            col[0] = top_n

        each(0, NB, logit_step)
        col[0] = jnp.broadcast_to(jnp.max(col[0], axis=1, keepdims=True), (GR, 128))

        def exp_step(n):
            total_n = col[1]
            for i in range(BW // 128):
                a = jnp.exp(e_v[n, rows, i * 128 : (i + 1) * 128] - col[0])
                e_v[n, rows, i * 128 : (i + 1) * 128] = a
                total_n = total_n + a
            col[1] = total_n

        each(0, NB, exp_step)
        sums = jnp.broadcast_to(jnp.sum(col[1], axis=1, keepdims=True), (GR, 128))
        lane_t = lax.broadcasted_iota(jnp.int32, (GR, 128), 1)
        stats = jnp.where(lane_t == 0, col[0], sums).T[:8, :]
        for i in range(2):
            stx[group, i : i + 1, :] = stats[0:1, i * 128 : (i + 1) * 128]
            stx[group, 2 + i : 3 + i, :] = stats[1:2, i * 128 : (i + 1) * 128]
        stx[group, 4:, :] = jnp.zeros((4, 128), F32)
        sbuf[y_of(group), vc] = stx[group]
        each(1, VOC, lambda j: st(group, j, vc).start())

    def transposed_trunk(group):
        rows = group_rows(group)
        for half in range(2):
            for k in range(HALF // CW):
                ht[half * HALF + k * CW : half * HALF + (k + 1) * CW, rows] = (
                    hb[half, rows, k * CW : (k + 1) * CW].T
                )

    student(0)
    transposed_trunk(0)
    student(1)

    each(1, VOC, lambda j: tst(j, voc_from(j)).wait_recv())
    for i in range(4):
        rows = jnp.concatenate([tstat[4 * i + k][:, :ROWS] for k in range(4)], axis=1)
        rows = jnp.concatenate([rows, jnp.zeros((120, 128), F32)]).T
        tcol[0, i * 128 : (i + 1) * 128, :] = jnp.broadcast_to(rows[:, 0:1], (128, 128))
        tcol[1, i * 128 : (i + 1) * 128, :] = jnp.broadcast_to(rows[:, 1:2], (128, 128))

    def grad(group):
        rows = group_rows(group)
        each(1, VOC, lambda j: st(group, j, voc_from(j)).wait_recv())
        tops = [sbuf[y_of(group), i][:2] for i in range(VOC)]
        parts = [sbuf[y_of(group), i][2:4] for i in range(VOC)]
        top_all = tops[0]
        for x in tops[1:]:
            top_all = jnp.maximum(top_all, x)
        total_all = jnp.zeros_like(top_all)
        for x, y in zip(tops, parts):
            total_all = total_all + y * jnp.exp(x - top_all)
        factor = jnp.exp(stx[group][:2] - top_all) / total_all
        for i in range(2):
            col[0, i * 128 : (i + 1) * 128, :] = jnp.broadcast_to(factor[i : i + 1], (128, 128)).T
        if group == 0:
            own_tile.wait()
        near = 8 * group
        each(max(near, 1), near + 8, lambda j: a2a(j, tile_from(j), tile_to(j)).wait_recv())

        def grad_step(n):
            for side in range(BW // 128):
                cols = pl.ds(pl.multiple_of(n * BW + side * 128, 128), 128)
                teacher = jnp.exp(tbuf[rows, cols].astype(F32) - tcol[0, rows, :]) * tcol[1, rows, :]
                student = e_v[n, rows, side * 128 : side * 128 + 128] * col[0]
                lg_v[rows, cols] = (student - teacher).astype(BF16)

        each(0, NB, grad_step)

    def share(group, half, k):
        at = pl.ds(pl.multiple_of(half * HALF + k * BW, BW), BW)
        return lax.dot_general(
            lg_v[group_rows(group), :], w_v[at, :], (((1,), (1,)), ((), ())), preferred_element_type=F32
        )

    def x0(group, k):
        at = DK * group + k
        return remote(x0s.at[at], x0r.at[at], sx.at[at], rx.at[at], vocab=sib)

    def a1(group, j):
        at = 4 * group + j
        return remote(
            a1s.at[group, lax.rem(x_at + j, 4)], a1r.at[group, x_at], sa1.at[at], ra1.at[at], head=along_x(j)
        )

    def b1(y, j, src):
        at = CHIPS * y + j
        return remote(
            b1s.at[src, chip_at(j)], b1r.at[y, chip], sb1.at[at], rb1.at[at], vocab=2 * chip_at(j) + core
        )

    def b2(j):
        to = lax.rem(hd + j, HEAD)
        return remote(b2s.at[to], b2r.at[hd], sb2.at[j], rb2.at[j], head=to)

    def chip_at(j):
        return lax.rem(chip + CHIPS + j, CHIPS)

    def give(group, k):
        x0s[DK * group + k] = share(group, 1 - core, k).astype(BF16)
        x0(group, k).start()

    def both_cores(group, k):
        at = DK * group + k
        mine = share(group, core, k)
        x0(group, k).wait_recv()
        return mine + x0r[at].astype(F32)

    def shares(group):
        give(group, 0)
        give(group, 1)
        mine = both_cores(group, 0)
        for x in range(4):
            a1s[group, x] = mine[x * HR : (x + 1) * HR].astype(BF16)
        for j in (2, 1, 3):
            a1(group, j).start()
        a1r[group, x_at] = a1s[group, x_at]
        mine = both_cores(group, 1).reshape(4, CHIPS, 8, BW)
        for q in range(CHIPS):
            b1s[group, q] = mine[:, q].reshape(32, BW).astype(BF16)
        each(1, CHIPS, lambda j: b1(y_of(group), j, group).start())
        b1r[y_of(group), chip] = b1s[group, chip]

    def a2(group, p, j, owner_y, owner_chip):
        at = CHIPS * p + j
        return remote(
            a2s.at[group, chip_at(j)], a2r.at[owner_y, owner_chip], sa2.at[at], ra2.at[at],
            head=beside(p), vocab=2 * chip_at(j) + core,
        )

    def pass_sums(group):
        for j in range(1, 4):
            a1(group, j).wait_recv()
        total = a1r[group, 0].astype(F32)
        for x in range(1, 4):
            total = total + a1r[group, x].astype(F32)
        a2s[group] = total.reshape(CHIPS, 8, BW)
        p = lax.rem(y_of(group) + y_lo, 2)
        each(1, CHIPS, lambda j: a2(group, p, j, y_lo, chip).start())

        @pl.when(p == 1)
        def _():
            a2(group, p, 0, y_lo, chip).start()

        @pl.when(p == 0)
        def _():
            a2r[y_lo, chip] = a2s[group, chip]

    def pass_other_sums():
        for y in range(2):
            each(1, CHIPS, lambda j: b1(y, j, 0).wait_recv())
            total = b1r[y, 0].astype(F32)
            for q in range(1, CHIPS):
                total = total + b1r[y, q].astype(F32)
            b2s[4 * y : 4 * y + 4] = total.reshape(4, 8, BW)
        each(1, HEAD, lambda j: b2(j).start())
        b2r[hd] = b2s[hd]

    def weight_step(n):
        rows = pl.ds(pl.multiple_of(n * CW, CW), CW)
        wg_v[rows, :] = jnp.dot(ht[rows, :], lg_v[...], preferred_element_type=F32).astype(BF16)

    grad(0)
    shares(0)
    grad(1)
    shares(1)
    pass_sums(0)
    transposed_trunk(1)
    each(0, WG_FIRST, weight_step)
    pass_sums(1)
    pass_other_sums()
    each(WG_FIRST, NC, weight_step)

    for p in range(2):
        each(1 - p, CHIPS, lambda j: a2(0, p, j, lax.rem(y_lo + p, 2), chip_at(-j)).wait_recv())
    total = jnp.zeros((8, BW), F32)
    for p in range(2):
        for q in range(CHIPS):
            total = total + a2r[p, q]
    r3s[:, :BW] = total
    each(1, HEAD, lambda j: b2(j).wait_recv())
    total = b2r[0]
    for i in range(1, HEAD):
        total = total + b2r[i]
    r3s[:, BW:] = total
    mine = r3s[...]
    rs3 = remote(r3s, r3r, sr3, rr3, vocab=sib)
    rs3.start()
    rs3.wait_recv()
    other = r3r[...]
    first = core == 0
    low = jnp.where(first, mine, other)
    high = jnp.where(first, other, mine)
    out_ref[:, :HALF] = jnp.where(first, low[:4], low[4:])
    out_ref[:, HALF:] = jnp.where(first, high[:4], high[4:])

    for p in range(2):
        each(1 - p, VOC, lambda j: ag1(p, j, VOC * y_lo + vc, voc(j)).wait_send())
    each(1, VOC, lambda j: a2a(j, vc, tile_to(j)).wait_send())
    each(1, VOC, lambda j: tst(j, vc).wait_send())
    for group in range(2):
        each(1, VOC, lambda j: st(group, j, vc).wait_send())
    each(1, 4, lambda j: agx(1, j, 0).wait_send())
    for p in range(2):
        each(0, 4, lambda j: fwd(p, j, core).wait_send())
    for group in range(2):
        each(0, DK, lambda k: x0(group, k).wait_send())
        each(1, 4, lambda j: a1(group, j).wait_send())
        each(1, CHIPS, lambda j: b1(group, j, 0).wait_send())
    each(1, HEAD, lambda j: b2(j).wait_send())
    for p in range(2):
        each(1 - p, CHIPS, lambda j: a2(0, p, j, y_lo, chip).wait_send())
    rs3.wait_send()


def per_device(hidden_rows, head_weight, teacher_logits):
    hbm = pl.BlockSpec(memory_space=pltpu.MemorySpace.HBM)
    vmem = pl.BlockSpec(memory_space=pltpu.VMEM)
    dma = pltpu.SemaphoreType.DMA
    weight_grad, input_grad = pl.pallas_call(
        kernel,
        out_shape=(
            pltpu.VMEM((D, COLS), BF16),
            jax.ShapeDtypeStruct((TOK // (HEAD * VOC), D), F32),
        ),
        in_specs=[vmem, hbm, hbm],
        out_specs=(vmem, vmem),
        scratch_shapes=[
            pltpu.VMEM((D, COLS), BF16),
            pltpu.VMEM((ROWS, COLS * VOC), BF16),
            pltpu.VMEM((TOK, COLS), BF16),
            pltpu.VMEM((16, CW), F32),
            pltpu.VMEM((2, 16, CW), BF16),
            pltpu.VMEM((2 * VOC, 16, CW), BF16),
            pltpu.VMEM((HR, HALF), F32),
            pltpu.VMEM((2, TOK, HALF), BF16),
            pltpu.VMEM((D, TOK), BF16),
            pltpu.VMEM((NB, TOK, BW), F32),
            pltpu.VMEM((TOK, COLS), BF16),
            pltpu.VMEM((2, GR, 128), F32),
            pltpu.VMEM((2, TOK, 128), F32),
            pltpu.VMEM((8, 128), F32),
            pltpu.VMEM((VOC, 8, 128), F32),
            pltpu.VMEM((2, 8, 128), F32),
            pltpu.VMEM((2, VOC, 8, 128), F32),
            pltpu.VMEM((2 * DK, GR, BW), BF16),
            pltpu.VMEM((2 * DK, GR, BW), BF16),
            pltpu.VMEM((2, 4, HR, BW), BF16),
            pltpu.VMEM((2, 4, HR, BW), BF16),
            pltpu.VMEM((2, CHIPS, 8, BW), F32),
            pltpu.VMEM((2, CHIPS, 8, BW), F32),
            pltpu.VMEM((2, CHIPS, 32, BW), BF16),
            pltpu.VMEM((2, CHIPS, 32, BW), BF16),
            pltpu.VMEM((HEAD, 8, BW), F32),
            pltpu.VMEM((HEAD, 8, BW), F32),
            pltpu.VMEM((8, HALF), F32),
            pltpu.VMEM((8, HALF), F32),
            dma((3,)),
            dma((2 * VOC,)), dma((2 * VOC,)), dma((VOC,)), dma((VOC,)), dma((VOC,)), dma((VOC,)),
            dma((8,)), dma((8,)), dma((8,)), dma((8,)),
            dma((2 * VOC,)), dma((2 * VOC,)), dma((2 * DK,)), dma((2 * DK,)),
            dma((8,)), dma((8,)), dma((2 * CHIPS,)), dma((2 * CHIPS,)),
            dma((2 * CHIPS,)), dma((2 * CHIPS,)), dma((HEAD,)), dma((HEAD,)), dma, dma,
        ],
        compiler_params=pltpu.CompilerParams(
            collective_id=0, has_side_effects=True, vmem_limit_bytes=44 * 1024 * 1024
        ),
        cost_estimate=pl.CostEstimate(
            flops=6 * TOK * D * COLS, bytes_accessed=20 * 1024 * 1024, transcendentals=3 * TOK * COLS
        ),
    )(hidden_rows, head_weight[0], teacher_logits[0])
    return weight_grad[None], input_grad


def solution(mesh):
    return jax.shard_map(
        per_device,
        mesh=mesh,
        in_specs=(P(("head", "vocab"), None), P("head", None, "vocab"), P("head", "vocab", None)),
        out_specs=(P("head", None, "vocab"), P(("head", "vocab"), None)),
        check_vma=False,
    )
```

```python
import jax
import jax.numpy as jnp
from jax import lax
from jax.experimental import pallas as pl
from jax.experimental.pallas import tpu as pltpu
from jax.sharding import PartitionSpec as P

MESH = pl.DeviceIdType.MESH
F32, BF16 = jnp.float32, jnp.bfloat16
HEAD, VOC, CHIPS = 8, 16, 8
D, TOK, COLS = 2048, 512, 2048
ROWS = TOK // VOC
HR = TOK // HEAD
HALF = D // 2
CW = 256
NC = COLS // CW
BW = 512
NB = COLS // BW
GR = TOK // 2
WG_FIRST = 3
DK = HALF // BW


def kernel(
    h_hbm, w_hbm, t_hbm, wg_v, out_ref,
    h_v, w_v, t_v, tbuf, pack, own, st1, hs, hb, ht, e_v, lg_v,
    col, tcol, tst_src, tstat, stx, sbuf, x0s, x0r,
    a1s, a1r, a2s, a2r, b1s, b1r, b2s, b2r, r3s, r3r,
    local_sem,
    s1, r1, sa, ra, stt, rtt, s2, r2, sf, rf, sst, rst, sx, rx,
    sa1, ra1, sa2, ra2, sb1, rb1, sb2, rb2, sr3, rr3,
):
    hd, vc = lax.axis_index("head"), lax.axis_index("vocab")
    chip = vc // 2
    core = vc - 2 * chip
    sib = 2 * chip + 1 - core

    def rows_of(index, count):
        return pl.ds(pl.multiple_of(index * count, count), count)

    def each(start, stop, body):
        def step(j, carry):
            body(j)
            return carry
        lax.fori_loop(start, stop, step, 0)

    def voc(j):
        return lax.rem(vc + j, VOC)

    def voc_from(j):
        return lax.rem(vc + VOC - j, VOC)

    y_hi, y_lo = vc // 8, hd // 4
    x_at = hd - 4 * y_lo

    def y_of(group):
        return lax.rem(y_hi + group, 2)

    def head_at(group, j):
        return 4 * y_of(group) + lax.rem(x_at + 4 + j, 4)

    def beside(p):
        return 4 * lax.rem(y_lo + p, 2) + x_at

    def along_x(j):
        return 4 * y_lo + lax.rem(x_at + j, 4)

    def remote(src, dst, send, recv, **to):
        return pltpu.make_async_remote_copy(
            src_ref=src, dst_ref=dst, send_sem=send, recv_sem=recv, device_id=to, device_id_type=MESH
        )

    w_copy = pltpu.make_async_copy(w_hbm, w_v, local_sem.at[0])
    t_copy = pltpu.make_async_copy(t_hbm, t_v, local_sem.at[1])
    own_tile = pltpu.make_async_copy(
        t_hbm.at[:, rows_of(vc, COLS)], tbuf.at[rows_of(vc, ROWS), :], local_sem.at[2]
    )
    h_copy = pltpu.make_async_copy(h_hbm, h_v, local_sem.at[3])
    h_copy.start()
    t_copy.start()
    w_copy.start()
    own_tile.start()
    barrier = pltpu.get_barrier_semaphore()

    def greet(**to):
        pl.semaphore_signal(barrier, inc=1, device_id=to, device_id_type=MESH)

    each(1, VOC, lambda j: greet(vocab=voc(j)))
    each(0, VOC, lambda j: greet(head=beside(1), vocab=voc(j)))
    each(1, 4, lambda j: greet(head=along_x(j)))
    each(1, 4, lambda j: greet(head=4 * lax.rem(y_lo + 1, 2) + lax.rem(x_at + j, 4)))
    h_copy.wait()
    for side in range(2):
        for g in range(4):
            at = side * HALF + g * CW
            pack[4 * g : 4 * g + 4, :] = h_v[:, at : at + CW].astype(F32)
        own[side] = pack[...].astype(BF16)
    pl.semaphore_wait(barrier, 2 * VOC - 1 + 6)

    def ag1(p, j, owner, to):
        return remote(
            own.at[lax.rem(to, 2)], st1.at[owner], s1.at[VOC * p + j], r1.at[VOC * p + j],
            head=beside(p), vocab=to,
        )

    each(1, VOC, lambda j: ag1(0, j, VOC * y_lo + vc, voc(j)).start())
    each(0, VOC, lambda j: ag1(1, j, VOC * y_lo + vc, voc(j)).start())

    def tile_to(j):
        return 8 * lax.rem(y_hi + j // 8, 2) + lax.rem(vc + j, 8)

    def tile_from(j):
        return 8 * lax.rem(y_hi + j // 8, 2) + lax.rem(vc + 16 - j, 8)

    def a2a(j, owner, to):
        return remote(
            t_hbm.at[:, rows_of(to, COLS)], tbuf.at[rows_of(owner, ROWS), :], sa.at[j], ra.at[j], vocab=to
        )

    each(8, VOC, lambda j: a2a(j, vc, tile_to(j)).start())
    each(1, 8, lambda j: a2a(j, vc, tile_to(j)).start())

    def block(side, p, j):
        return hb.at[side, rows_of(head_at(p, j), HR), :]

    def agx(p, j, src):
        return remote(
            block(core, p, src), block(core, p, src), s2.at[4 * p + j], r2.at[4 * p + j], head=along_x(j)
        )

    def fwd(p, j, side):
        at = block(side, p, -j)
        return remote(at, at, sf.at[4 * p + j], rf.at[4 * p + j], vocab=sib)

    t_copy.wait()
    TW = 2048

    def top_step(i, top):
        x = t_v[:, pl.ds(pl.multiple_of(i * TW, TW), TW)].astype(F32)
        for k in range(TW // 128):
            top = jnp.maximum(top, x[:, k * 128 : (k + 1) * 128])
        return top

    top = lax.fori_loop(0, COLS * VOC // TW, top_step, jnp.full((ROWS, 128), -jnp.inf, F32))
    top = jnp.broadcast_to(jnp.max(top, axis=1, keepdims=True), (ROWS, 128))

    def sum_step(i, total):
        x = t_v[:, pl.ds(pl.multiple_of(i * TW, TW), TW)].astype(F32)
        for k in range(TW // 128):
            total = total + jnp.exp(x[:, k * 128 : (k + 1) * 128] - top)
        return total

    total = lax.fori_loop(0, COLS * VOC // TW, sum_step, jnp.zeros((ROWS, 128), F32))
    scale = 1.0 / jnp.broadcast_to(jnp.sum(total, axis=1, keepdims=True), (ROWS, 128))
    lane = lax.broadcasted_iota(jnp.int32, (ROWS, 128), 1)
    both = jnp.concatenate([jnp.where(lane == 0, top, scale), jnp.zeros((128 - ROWS, 128), F32)])
    tst_src[...] = both.T[:8]
    tstat[vc] = tst_src[...]

    def tst(j, owner):
        return remote(tst_src, tstat.at[owner], stt.at[j], rtt.at[j], vocab=voc(j))

    each(1, VOC, lambda j: tst(j, vc).start())

    st1[VOC * y_lo + vc] = own[core]
    for p in range(2):
        each(1 - p, VOC, lambda j: ag1(p, j, VOC * lax.rem(y_lo + p, 2) + voc_from(j), voc(j)).wait_recv())
    for group in range(2):
        for i in range(VOC):
            rows = st1[VOC * y_of(group) + i].astype(F32)
            for g in range(4):
                hs[4 * i : 4 * i + 4, g * CW : (g + 1) * CW] = rows[4 * g : 4 * g + 4, :]
        hb[core, rows_of(head_at(group, 0), HR), :] = hs[...].astype(BF16)
        if group == 0:
            for j in (1, 3, 2):
                agx(0, j, 0).start()
        fwd(group, 0, core).start()

    def group_rows(group):
        return rows_of(y_of(group), GR)

    def st(group, j, owner):
        at = VOC * y_of(group) + j
        return remote(stx.at[group], sbuf.at[y_of(group), owner], sst.at[at], rst.at[at], vocab=voc(j))

    def student(group):
        rows = group_rows(group)
        if group == 0:
            each(1, 4, lambda j: agx(0, j, 0).wait_send())
            for j in (1, 3, 2):
                agx(1, j, 0).start()
        for j in (1, 3, 2):
            agx(group, j, -j).wait_recv()
            fwd(group, j, core).start()
        each(0, 4, lambda j: fwd(group, j, 1 - core).wait_recv())
        if group == 0:
            w_copy.wait()
        col[0] = jnp.full((GR, 128), -jnp.inf, F32)
        col[1] = jnp.zeros((GR, 128), F32)

        def logit_step(n):
            cols = pl.ds(pl.multiple_of(n * BW, BW), BW)
            x = jnp.dot(hb[0, rows, :], w_v[:HALF, cols], preferred_element_type=F32)
            x = x + jnp.dot(hb[1, rows, :], w_v[HALF:, cols], preferred_element_type=F32)
            e_v[n, rows, :] = x
            top_n = col[0]
            for i in range(BW // 128):
                top_n = jnp.maximum(top_n, x[:, i * 128 : (i + 1) * 128])
            col[0] = top_n

        each(0, NB, logit_step)
        col[0] = jnp.broadcast_to(jnp.max(col[0], axis=1, keepdims=True), (GR, 128))

        def exp_step(n):
            total_n = col[1]
            for i in range(BW // 128):
                a = jnp.exp(e_v[n, rows, i * 128 : (i + 1) * 128] - col[0])
                e_v[n, rows, i * 128 : (i + 1) * 128] = a
                total_n = total_n + a
            col[1] = total_n

        each(0, NB, exp_step)
        sums = jnp.broadcast_to(jnp.sum(col[1], axis=1, keepdims=True), (GR, 128))
        lane_t = lax.broadcasted_iota(jnp.int32, (GR, 128), 1)
        stats = jnp.where(lane_t == 0, col[0], sums).T[:8, :]
        for i in range(2):
            stx[group, i : i + 1, :] = stats[0:1, i * 128 : (i + 1) * 128]
            stx[group, 2 + i : 3 + i, :] = stats[1:2, i * 128 : (i + 1) * 128]
        stx[group, 4:, :] = jnp.zeros((4, 128), F32)
        sbuf[y_of(group), vc] = stx[group]
        each(1, VOC, lambda j: st(group, j, vc).start())

    def transposed_trunk(group):
        rows = group_rows(group)
        for half in range(2):
            for k in range(HALF // CW):
                ht[half * HALF + k * CW : half * HALF + (k + 1) * CW, rows] = (
                    hb[half, rows, k * CW : (k + 1) * CW].T
                )

    student(0)
    transposed_trunk(0)
    student(1)

    each(1, VOC, lambda j: tst(j, voc_from(j)).wait_recv())
    for i in range(4):
        rows = jnp.concatenate([tstat[4 * i + k][:, :ROWS] for k in range(4)], axis=1)
        rows = jnp.concatenate([rows, jnp.zeros((120, 128), F32)]).T
        tcol[0, i * 128 : (i + 1) * 128, :] = jnp.broadcast_to(rows[:, 0:1], (128, 128))
        tcol[1, i * 128 : (i + 1) * 128, :] = jnp.broadcast_to(rows[:, 1:2], (128, 128))

    def grad(group):
        rows = group_rows(group)
        each(1, VOC, lambda j: st(group, j, voc_from(j)).wait_recv())
        tops = [sbuf[y_of(group), i][:2] for i in range(VOC)]
        parts = [sbuf[y_of(group), i][2:4] for i in range(VOC)]
        top_all = tops[0]
        for x in tops[1:]:
            top_all = jnp.maximum(top_all, x)
        total_all = jnp.zeros_like(top_all)
        for x, y in zip(tops, parts):
            total_all = total_all + y * jnp.exp(x - top_all)
        factor = jnp.exp(stx[group][:2] - top_all) / total_all
        for i in range(2):
            col[0, i * 128 : (i + 1) * 128, :] = jnp.broadcast_to(factor[i : i + 1], (128, 128)).T
        if group == 0:
            own_tile.wait()
        near = 8 * group
        each(max(near, 1), near + 8, lambda j: a2a(j, tile_from(j), tile_to(j)).wait_recv())

        def grad_step(n):
            for side in range(BW // 128):
                cols = pl.ds(pl.multiple_of(n * BW + side * 128, 128), 128)
                teacher = jnp.exp(tbuf[rows, cols].astype(F32) - tcol[0, rows, :]) * tcol[1, rows, :]
                student = e_v[n, rows, side * 128 : side * 128 + 128] * col[0]
                lg_v[rows, cols] = (student - teacher).astype(BF16)

        each(0, NB, grad_step)

    def share(group, half, k):
        at = pl.ds(pl.multiple_of(half * HALF + k * BW, BW), BW)
        return lax.dot_general(
            lg_v[group_rows(group), :], w_v[at, :], (((1,), (1,)), ((), ())), preferred_element_type=F32
        )

    def x0(group, k):
        at = DK * group + k
        return remote(x0s.at[at], x0r.at[at], sx.at[at], rx.at[at], vocab=sib)

    def a1(group, j):
        at = 4 * group + j
        return remote(
            a1s.at[group, lax.rem(x_at + j, 4)], a1r.at[group, x_at], sa1.at[at], ra1.at[at], head=along_x(j)
        )

    def b1(y, j, src):
        at = CHIPS * y + j
        return remote(
            b1s.at[src, chip_at(j)], b1r.at[y, chip], sb1.at[at], rb1.at[at], vocab=2 * chip_at(j) + core
        )

    def b2(j):
        to = lax.rem(hd + j, HEAD)
        return remote(b2s.at[to], b2r.at[hd], sb2.at[j], rb2.at[j], head=to)

    def chip_at(j):
        return lax.rem(chip + CHIPS + j, CHIPS)

    def give(group, k):
        x0s[DK * group + k] = share(group, 1 - core, k).astype(BF16)
        x0(group, k).start()

    def both_cores(group, k):
        at = DK * group + k
        mine = share(group, core, k)
        x0(group, k).wait_recv()
        return mine + x0r[at].astype(F32)

    def shares(group):
        give(group, 0)
        give(group, 1)
        mine = both_cores(group, 0)
        for x in range(4):
            a1s[group, x] = mine[x * HR : (x + 1) * HR].astype(BF16)
        for j in (2, 1, 3):
            a1(group, j).start()
        a1r[group, x_at] = a1s[group, x_at]
        mine = both_cores(group, 1).reshape(4, CHIPS, 8, BW)
        for q in range(CHIPS):
            b1s[group, q] = mine[:, q].reshape(32, BW).astype(BF16)
        each(1, CHIPS, lambda j: b1(y_of(group), j, group).start())
        b1r[y_of(group), chip] = b1s[group, chip]

    def a2(group, p, j, owner_y, owner_chip):
        at = CHIPS * p + j
        return remote(
            a2s.at[group, chip_at(j)], a2r.at[owner_y, owner_chip], sa2.at[at], ra2.at[at],
            head=beside(p), vocab=2 * chip_at(j) + core,
        )

    def pass_sums(group):
        for j in range(1, 4):
            a1(group, j).wait_recv()
        total = a1r[group, 0].astype(F32)
        for x in range(1, 4):
            total = total + a1r[group, x].astype(F32)
        a2s[group] = total.reshape(CHIPS, 8, BW)
        p = lax.rem(y_of(group) + y_lo, 2)
        each(1, CHIPS, lambda j: a2(group, p, j, y_lo, chip).start())

        @pl.when(p == 1)
        def _():
            a2(group, p, 0, y_lo, chip).start()

        @pl.when(p == 0)
        def _():
            a2r[y_lo, chip] = a2s[group, chip]

    def pass_other_sums():
        for y in range(2):
            each(1, CHIPS, lambda j: b1(y, j, 0).wait_recv())
            total = b1r[y, 0].astype(F32)
            for q in range(1, CHIPS):
                total = total + b1r[y, q].astype(F32)
            b2s[4 * y : 4 * y + 4] = total.reshape(4, 8, BW)
        each(1, HEAD, lambda j: b2(j).start())
        b2r[hd] = b2s[hd]

    def weight_step(n):
        rows = pl.ds(pl.multiple_of(n * CW, CW), CW)
        wg_v[rows, :] = jnp.dot(ht[rows, :], lg_v[...], preferred_element_type=F32).astype(BF16)

    grad(0)
    shares(0)
    grad(1)
    pass_sums(0)
    shares(1)
    transposed_trunk(1)
    each(0, WG_FIRST, weight_step)
    pass_sums(1)
    pass_other_sums()
    each(WG_FIRST, NC, weight_step)

    for p in range(2):
        each(1 - p, CHIPS, lambda j: a2(0, p, j, lax.rem(y_lo + p, 2), chip_at(-j)).wait_recv())
    total = jnp.zeros((8, BW), F32)
    for p in range(2):
        for q in range(CHIPS):
            total = total + a2r[p, q]
    r3s[:, :BW] = total
    each(1, HEAD, lambda j: b2(j).wait_recv())
    total = b2r[0]
    for i in range(1, HEAD):
        total = total + b2r[i]
    r3s[:, BW:] = total
    mine = r3s[...]
    rs3 = remote(r3s, r3r, sr3, rr3, vocab=sib)
    rs3.start()
    rs3.wait_recv()
    other = r3r[...]
    first = core == 0
    low = jnp.where(first, mine, other)
    high = jnp.where(first, other, mine)
    out_ref[:, :HALF] = jnp.where(first, low[:4], low[4:])
    out_ref[:, HALF:] = jnp.where(first, high[:4], high[4:])

    for p in range(2):
        each(1 - p, VOC, lambda j: ag1(p, j, VOC * y_lo + vc, voc(j)).wait_send())
    each(1, VOC, lambda j: a2a(j, vc, tile_to(j)).wait_send())
    each(1, VOC, lambda j: tst(j, vc).wait_send())
    for group in range(2):
        each(1, VOC, lambda j: st(group, j, vc).wait_send())
    each(1, 4, lambda j: agx(1, j, 0).wait_send())
    for p in range(2):
        each(0, 4, lambda j: fwd(p, j, core).wait_send())
    for group in range(2):
        each(0, DK, lambda k: x0(group, k).wait_send())
        each(1, 4, lambda j: a1(group, j).wait_send())
        each(1, CHIPS, lambda j: b1(group, j, 0).wait_send())
    each(1, HEAD, lambda j: b2(j).wait_send())
    for p in range(2):
        each(1 - p, CHIPS, lambda j: a2(0, p, j, y_lo, chip).wait_send())
    rs3.wait_send()


def per_device(hidden_rows, head_weight, teacher_logits):
    hbm = pl.BlockSpec(memory_space=pltpu.MemorySpace.HBM)
    vmem = pl.BlockSpec(memory_space=pltpu.VMEM)
    dma = pltpu.SemaphoreType.DMA
    weight_grad, input_grad = pl.pallas_call(
        kernel,
        out_shape=(
            pltpu.VMEM((D, COLS), BF16),
            jax.ShapeDtypeStruct((TOK // (HEAD * VOC), D), F32),
        ),
        in_specs=[hbm, hbm, hbm],
        out_specs=(vmem, vmem),
        scratch_shapes=[
            pltpu.VMEM((TOK // (HEAD * VOC), D), BF16),
            pltpu.VMEM((D, COLS), BF16),
            pltpu.VMEM((ROWS, COLS * VOC), BF16),
            pltpu.VMEM((TOK, COLS), BF16),
            pltpu.VMEM((16, CW), F32),
            pltpu.VMEM((2, 16, CW), BF16),
            pltpu.VMEM((2 * VOC, 16, CW), BF16),
            pltpu.VMEM((HR, HALF), F32),
            pltpu.VMEM((2, TOK, HALF), BF16),
            pltpu.VMEM((D, TOK), BF16),
            pltpu.VMEM((NB, TOK, BW), F32),
            pltpu.VMEM((TOK, COLS), BF16),
            pltpu.VMEM((2, GR, 128), F32),
            pltpu.VMEM((2, TOK, 128), F32),
            pltpu.VMEM((8, 128), F32),
            pltpu.VMEM((VOC, 8, 128), F32),
            pltpu.VMEM((2, 8, 128), F32),
            pltpu.VMEM((2, VOC, 8, 128), F32),
            pltpu.VMEM((2 * DK, GR, BW), BF16),
            pltpu.VMEM((2 * DK, GR, BW), BF16),
            pltpu.VMEM((2, 4, HR, BW), BF16),
            pltpu.VMEM((2, 4, HR, BW), BF16),
            pltpu.VMEM((2, CHIPS, 8, BW), F32),
            pltpu.VMEM((2, CHIPS, 8, BW), F32),
            pltpu.VMEM((2, CHIPS, 32, BW), BF16),
            pltpu.VMEM((2, CHIPS, 32, BW), BF16),
            pltpu.VMEM((HEAD, 8, BW), F32),
            pltpu.VMEM((HEAD, 8, BW), F32),
            pltpu.VMEM((8, HALF), F32),
            pltpu.VMEM((8, HALF), F32),
            dma((4,)),
            dma((2 * VOC,)), dma((2 * VOC,)), dma((VOC,)), dma((VOC,)), dma((VOC,)), dma((VOC,)),
            dma((8,)), dma((8,)), dma((8,)), dma((8,)),
            dma((2 * VOC,)), dma((2 * VOC,)), dma((2 * DK,)), dma((2 * DK,)),
            dma((8,)), dma((8,)), dma((2 * CHIPS,)), dma((2 * CHIPS,)),
            dma((2 * CHIPS,)), dma((2 * CHIPS,)), dma((HEAD,)), dma((HEAD,)), dma, dma,
        ],
        compiler_params=pltpu.CompilerParams(
            collective_id=0, has_side_effects=True, vmem_limit_bytes=44 * 1024 * 1024
        ),
        cost_estimate=pl.CostEstimate(
            flops=6 * TOK * D * COLS, bytes_accessed=20 * 1024 * 1024, transcendentals=3 * TOK * COLS
        ),
    )(hidden_rows, head_weight[0], teacher_logits[0])
    return weight_grad[None], input_grad


def solution(mesh):
    return jax.shard_map(
        per_device,
        mesh=mesh,
        in_specs=(P(("head", "vocab"), None), P("head", None, "vocab"), P("head", "vocab", None)),
        out_specs=(P("head", None, "vocab"), P(("head", "vocab"), None)),
        check_vma=False,
    )
```

```python
import jax
import jax.numpy as jnp
from jax import lax
from jax.experimental import pallas as pl
from jax.experimental.pallas import tpu as pltpu
from jax.sharding import PartitionSpec as P

MESH = pl.DeviceIdType.MESH
F32, BF16 = jnp.float32, jnp.bfloat16
HEAD, VOC, CHIPS = 8, 16, 8
D, TOK, COLS = 2048, 512, 2048
ROWS = TOK // VOC
HR = TOK // HEAD
HALF = D // 2
CW = 256
NC = COLS // CW
BW = 512
NB = COLS // BW
GR = TOK // 2
WG_FIRST = 3
DK = HALF // BW


def kernel(
    h_hbm, w_hbm, t_hbm, wg_v, out_ref,
    h_v, w_v, t_v, tbuf, pack, own, st1, hs, hb, ht, e_v, lg_v,
    col, tcol, tst_src, tstat, stx, sbuf, x0s, x0r,
    a1s, a1r, a2s, a2r, b1s, b1r, b2s, b2r, r3s, r3r,
    local_sem,
    s1, r1, sa, ra, stt, rtt, s2, r2, sf, rf, sst, rst, sx, rx,
    sa1, ra1, sa2, ra2, sb1, rb1, sb2, rb2, sr3, rr3,
):
    hd, vc = lax.axis_index("head"), lax.axis_index("vocab")
    chip = vc // 2
    core = vc - 2 * chip
    sib = 2 * chip + 1 - core

    def rows_of(index, count):
        return pl.ds(pl.multiple_of(index * count, count), count)

    def each(start, stop, body):
        def step(j, carry):
            body(j)
            return carry
        lax.fori_loop(start, stop, step, 0)

    def voc(j):
        return lax.rem(vc + j, VOC)

    def voc_from(j):
        return lax.rem(vc + VOC - j, VOC)

    y_hi, y_lo = vc // 8, hd // 4
    x_at = hd - 4 * y_lo

    def y_of(group):
        return lax.rem(y_hi + group, 2)

    def head_at(group, j):
        return 4 * y_of(group) + lax.rem(x_at + 4 + j, 4)

    def beside(p):
        return 4 * lax.rem(y_lo + p, 2) + x_at

    def along_x(j):
        return 4 * y_lo + lax.rem(x_at + j, 4)

    def remote(src, dst, send, recv, **to):
        return pltpu.make_async_remote_copy(
            src_ref=src, dst_ref=dst, send_sem=send, recv_sem=recv, device_id=to, device_id_type=MESH
        )

    w_copy = pltpu.make_async_copy(w_hbm, w_v, local_sem.at[0])
    t_copy = pltpu.make_async_copy(t_hbm, t_v, local_sem.at[1])
    own_tile = pltpu.make_async_copy(
        t_hbm.at[:, rows_of(vc, COLS)], tbuf.at[rows_of(vc, ROWS), :], local_sem.at[2]
    )
    h_copy = pltpu.make_async_copy(h_hbm, h_v, local_sem.at[3])
    h_copy.start()
    t_copy.start()
    w_copy.start()
    own_tile.start()
    barrier = pltpu.get_barrier_semaphore()

    def greet(**to):
        pl.semaphore_signal(barrier, inc=1, device_id=to, device_id_type=MESH)

    each(1, VOC, lambda j: greet(vocab=voc(j)))
    each(0, VOC, lambda j: greet(head=beside(1), vocab=voc(j)))
    each(1, 4, lambda j: greet(head=along_x(j)))
    each(1, 4, lambda j: greet(head=4 * lax.rem(y_lo + 1, 2) + lax.rem(x_at + j, 4)))
    h_copy.wait()
    for side in range(2):
        for g in range(4):
            at = side * HALF + g * CW
            pack[4 * g : 4 * g + 4, :] = h_v[:, at : at + CW].astype(F32)
        own[side] = pack[...].astype(BF16)
    pl.semaphore_wait(barrier, 2 * VOC - 1 + 6)

    def ag1(p, j, owner, to):
        return remote(
            own.at[lax.rem(to, 2)], st1.at[owner], s1.at[VOC * p + j], r1.at[VOC * p + j],
            head=beside(p), vocab=to,
        )

    each(1, VOC, lambda j: ag1(0, j, VOC * y_lo + vc, voc(j)).start())
    each(0, VOC, lambda j: ag1(1, j, VOC * y_lo + vc, voc(j)).start())

    def tile_to(j):
        return 8 * lax.rem(y_hi + j // 8, 2) + lax.rem(vc + j, 8)

    def tile_from(j):
        return 8 * lax.rem(y_hi + j // 8, 2) + lax.rem(vc + 16 - j, 8)

    def a2a(j, owner, to):
        return remote(
            t_hbm.at[:, rows_of(to, COLS)], tbuf.at[rows_of(owner, ROWS), :], sa.at[j], ra.at[j], vocab=to
        )

    each(8, VOC, lambda j: a2a(j, vc, tile_to(j)).start())
    each(1, 8, lambda j: a2a(j, vc, tile_to(j)).start())

    def block(side, p, j):
        return hb.at[side, rows_of(head_at(p, j), HR), :]

    def agx(p, j, src):
        return remote(
            block(core, p, src), block(core, p, src), s2.at[4 * p + j], r2.at[4 * p + j], head=along_x(j)
        )

    def fwd(p, j, side):
        at = block(side, p, -j)
        return remote(at, at, sf.at[4 * p + j], rf.at[4 * p + j], vocab=sib)

    t_copy.wait()
    TW = 2048

    def top_step(i, top):
        x = t_v[:, pl.ds(pl.multiple_of(i * TW, TW), TW)].astype(F32)
        for k in range(TW // 128):
            top = jnp.maximum(top, x[:, k * 128 : (k + 1) * 128])
        return top

    top = lax.fori_loop(0, COLS * VOC // TW, top_step, jnp.full((ROWS, 128), -jnp.inf, F32))
    top = jnp.broadcast_to(jnp.max(top, axis=1, keepdims=True), (ROWS, 128))

    def sum_step(i, total):
        x = t_v[:, pl.ds(pl.multiple_of(i * TW, TW), TW)].astype(F32)
        for k in range(TW // 128):
            total = total + jnp.exp(x[:, k * 128 : (k + 1) * 128] - top)
        return total

    total = lax.fori_loop(0, COLS * VOC // TW, sum_step, jnp.zeros((ROWS, 128), F32))
    scale = 1.0 / jnp.broadcast_to(jnp.sum(total, axis=1, keepdims=True), (ROWS, 128))
    lane = lax.broadcasted_iota(jnp.int32, (ROWS, 128), 1)
    both = jnp.concatenate([jnp.where(lane == 0, top, scale), jnp.zeros((128 - ROWS, 128), F32)])
    tst_src[...] = both.T[:8]
    tstat[vc] = tst_src[...]

    def tst(j, owner):
        return remote(tst_src, tstat.at[owner], stt.at[j], rtt.at[j], vocab=voc(j))

    each(1, VOC, lambda j: tst(j, vc).start())

    st1[VOC * y_lo + vc] = own[core]
    for p in range(2):
        each(1 - p, VOC, lambda j: ag1(p, j, VOC * lax.rem(y_lo + p, 2) + voc_from(j), voc(j)).wait_recv())
    for group in range(2):
        for i in range(VOC):
            rows = st1[VOC * y_of(group) + i].astype(F32)
            for g in range(4):
                hs[4 * i : 4 * i + 4, g * CW : (g + 1) * CW] = rows[4 * g : 4 * g + 4, :]
        hb[core, rows_of(head_at(group, 0), HR), :] = hs[...].astype(BF16)
        if group == 0:
            for j in (1, 3, 2):
                agx(0, j, 0).start()
        fwd(group, 0, core).start()

    def group_rows(group):
        return rows_of(y_of(group), GR)

    def st(group, j, owner):
        at = VOC * y_of(group) + j
        return remote(stx.at[group], sbuf.at[y_of(group), owner], sst.at[at], rst.at[at], vocab=voc(j))

    def student(group):
        rows = group_rows(group)
        if group == 0:
            each(1, 4, lambda j: agx(0, j, 0).wait_send())
            for j in (1, 3, 2):
                agx(1, j, 0).start()
        for j in (1, 3, 2):
            agx(group, j, -j).wait_recv()
            fwd(group, j, core).start()
        each(0, 4, lambda j: fwd(group, j, 1 - core).wait_recv())
        if group == 0:
            w_copy.wait()
        col[0] = jnp.full((GR, 128), -jnp.inf, F32)
        col[1] = jnp.zeros((GR, 128), F32)

        def logit_step(n):
            cols = pl.ds(pl.multiple_of(n * BW, BW), BW)
            x = jnp.dot(hb[0, rows, :], w_v[:HALF, cols], preferred_element_type=F32)
            x = x + jnp.dot(hb[1, rows, :], w_v[HALF:, cols], preferred_element_type=F32)
            e_v[n, rows, :] = x
            top_n = col[0]
            for i in range(BW // 128):
                top_n = jnp.maximum(top_n, x[:, i * 128 : (i + 1) * 128])
            col[0] = top_n

        each(0, NB, logit_step)
        col[0] = jnp.broadcast_to(jnp.max(col[0], axis=1, keepdims=True), (GR, 128))

        def exp_step(n):
            total_n = col[1]
            for i in range(BW // 128):
                a = jnp.exp(e_v[n, rows, i * 128 : (i + 1) * 128] - col[0])
                e_v[n, rows, i * 128 : (i + 1) * 128] = a
                total_n = total_n + a
            col[1] = total_n

        each(0, NB, exp_step)
        sums = jnp.broadcast_to(jnp.sum(col[1], axis=1, keepdims=True), (GR, 128))
        lane_t = lax.broadcasted_iota(jnp.int32, (GR, 128), 1)
        stats = jnp.where(lane_t == 0, col[0], sums).T[:8, :]
        for i in range(2):
            stx[group, i : i + 1, :] = stats[0:1, i * 128 : (i + 1) * 128]
            stx[group, 2 + i : 3 + i, :] = stats[1:2, i * 128 : (i + 1) * 128]
        stx[group, 4:, :] = jnp.zeros((4, 128), F32)
        sbuf[y_of(group), vc] = stx[group]
        each(1, VOC, lambda j: st(group, j, vc).start())

    def transposed_trunk(group):
        rows = group_rows(group)
        for half in range(2):
            for k in range(HALF // CW):
                ht[half * HALF + k * CW : half * HALF + (k + 1) * CW, rows] = (
                    hb[half, rows, k * CW : (k + 1) * CW].T
                )

    student(0)
    transposed_trunk(0)
    student(1)

    each(1, VOC, lambda j: tst(j, voc_from(j)).wait_recv())
    for i in range(4):
        rows = jnp.concatenate([tstat[4 * i + k][:, :ROWS] for k in range(4)], axis=1)
        rows = jnp.concatenate([rows, jnp.zeros((120, 128), F32)]).T
        tcol[0, i * 128 : (i + 1) * 128, :] = jnp.broadcast_to(rows[:, 0:1], (128, 128))
        tcol[1, i * 128 : (i + 1) * 128, :] = jnp.broadcast_to(rows[:, 1:2], (128, 128))

    def grad(group):
        rows = group_rows(group)
        each(1, VOC, lambda j: st(group, j, voc_from(j)).wait_recv())
        tops = [sbuf[y_of(group), i][:2] for i in range(VOC)]
        parts = [sbuf[y_of(group), i][2:4] for i in range(VOC)]
        top_all = tops[0]
        for x in tops[1:]:
            top_all = jnp.maximum(top_all, x)
        total_all = jnp.zeros_like(top_all)
        for x, y in zip(tops, parts):
            total_all = total_all + y * jnp.exp(x - top_all)
        factor = jnp.exp(stx[group][:2] - top_all) / total_all
        for i in range(2):
            col[0, i * 128 : (i + 1) * 128, :] = jnp.broadcast_to(factor[i : i + 1], (128, 128)).T
        if group == 0:
            own_tile.wait()
        near = 8 * group
        each(max(near, 1), near + 8, lambda j: a2a(j, tile_from(j), tile_to(j)).wait_recv())

        def grad_step(n):
            for side in range(BW // 128):
                cols = pl.ds(pl.multiple_of(n * BW + side * 128, 128), 128)
                teacher = jnp.exp(tbuf[rows, cols].astype(F32) - tcol[0, rows, :]) * tcol[1, rows, :]
                student = e_v[n, rows, side * 128 : side * 128 + 128] * col[0]
                lg_v[rows, cols] = (student - teacher).astype(BF16)

        each(0, NB, grad_step)

    def share(group, half, k):
        at = pl.ds(pl.multiple_of(half * HALF + k * BW, BW), BW)
        return lax.dot_general(
            lg_v[group_rows(group), :], w_v[at, :], (((1,), (1,)), ((), ())), preferred_element_type=F32
        )

    def x0(group, k):
        at = DK * group + k
        return remote(x0s.at[at], x0r.at[at], sx.at[at], rx.at[at], vocab=sib)

    def a1(group, j):
        at = 4 * group + j
        return remote(
            a1s.at[group, lax.rem(x_at + j, 4)], a1r.at[group, x_at], sa1.at[at], ra1.at[at], head=along_x(j)
        )

    def b1(y, j, src):
        at = CHIPS * y + j
        return remote(
            b1s.at[src, chip_at(j)], b1r.at[y, chip], sb1.at[at], rb1.at[at], vocab=2 * chip_at(j) + core
        )

    def b2(j):
        to = lax.rem(hd + j, HEAD)
        return remote(b2s.at[to], b2r.at[hd], sb2.at[j], rb2.at[j], head=to)

    def chip_at(j):
        return lax.rem(chip + CHIPS + j, CHIPS)

    def give(group, k):
        x0s[DK * group + k] = share(group, 1 - core, k).astype(BF16)
        x0(group, k).start()

    def both_cores(group, k):
        at = DK * group + k
        mine = share(group, core, k)
        x0(group, k).wait_recv()
        return mine + x0r[at].astype(F32)

    def shares(group):
        give(group, 0)
        give(group, 1)
        mine = both_cores(group, 0)
        for x in range(4):
            a1s[group, x] = mine[x * HR : (x + 1) * HR].astype(BF16)
        for j in (2, 1, 3):
            a1(group, j).start()
        a1r[group, x_at] = a1s[group, x_at]
        mine = both_cores(group, 1).reshape(4, CHIPS, 8, BW)
        for q in range(CHIPS):
            b1s[group, q] = mine[:, q].reshape(32, BW).astype(BF16)
        each(1, CHIPS, lambda j: b1(y_of(group), j, group).start())
        b1r[y_of(group), chip] = b1s[group, chip]

    def a2(group, p, j, owner_y, owner_chip):
        at = CHIPS * p + j
        return remote(
            a2s.at[group, chip_at(j)], a2r.at[owner_y, owner_chip], sa2.at[at], ra2.at[at],
            head=beside(p), vocab=2 * chip_at(j) + core,
        )

    def pass_sums(group):
        for j in range(1, 4):
            a1(group, j).wait_recv()
        total = a1r[group, 0].astype(F32)
        for x in range(1, 4):
            total = total + a1r[group, x].astype(F32)
        a2s[group] = total.reshape(CHIPS, 8, BW)
        p = lax.rem(y_of(group) + y_lo, 2)
        each(1, CHIPS, lambda j: a2(group, p, j, y_lo, chip).start())

        @pl.when(p == 1)
        def _():
            a2(group, p, 0, y_lo, chip).start()

        @pl.when(p == 0)
        def _():
            a2r[y_lo, chip] = a2s[group, chip]

    def pass_other_sums():
        for y in range(2):
            each(1, CHIPS, lambda j: b1(y, j, 0).wait_recv())
            total = b1r[y, 0].astype(F32)
            for q in range(1, CHIPS):
                total = total + b1r[y, q].astype(F32)
            b2s[4 * y : 4 * y + 4] = total.reshape(4, 8, BW)
        each(1, HEAD, lambda j: b2(j).start())
        b2r[hd] = b2s[hd]

    def weight_step(n):
        rows = pl.ds(pl.multiple_of(n * CW, CW), CW)
        wg_v[rows, :] = jnp.dot(ht[rows, :], lg_v[...], preferred_element_type=F32).astype(BF16)

    grad(0)
    shares(0)
    grad(1)
    shares(1)
    pass_sums(0)
    transposed_trunk(1)
    each(0, WG_FIRST, weight_step)
    pass_sums(1)
    pass_other_sums()
    each(WG_FIRST, NC, weight_step)

    for p in range(2):
        each(1 - p, CHIPS, lambda j: a2(0, p, j, lax.rem(y_lo + p, 2), chip_at(-j)).wait_recv())
    total = jnp.zeros((8, BW), F32)
    for p in range(2):
        for q in range(CHIPS):
            total = total + a2r[p, q]
    r3s[:, :BW] = total
    each(1, HEAD, lambda j: b2(j).wait_recv())
    total = b2r[0]
    for i in range(1, HEAD):
        total = total + b2r[i]
    r3s[:, BW:] = total
    mine = r3s[...]
    rs3 = remote(r3s, r3r, sr3, rr3, vocab=sib)
    rs3.start()
    rs3.wait_recv()
    other = r3r[...]
    first = core == 0
    low = jnp.where(first, mine, other)
    high = jnp.where(first, other, mine)
    out_ref[:, :HALF] = jnp.where(first, low[:4], low[4:])
    out_ref[:, HALF:] = jnp.where(first, high[:4], high[4:])

    for p in range(2):
        each(1 - p, VOC, lambda j: ag1(p, j, VOC * y_lo + vc, voc(j)).wait_send())
    each(1, VOC, lambda j: a2a(j, vc, tile_to(j)).wait_send())
    each(1, VOC, lambda j: tst(j, vc).wait_send())
    for group in range(2):
        each(1, VOC, lambda j: st(group, j, vc).wait_send())
    each(1, 4, lambda j: agx(1, j, 0).wait_send())
    for p in range(2):
        each(0, 4, lambda j: fwd(p, j, core).wait_send())
    for group in range(2):
        each(0, DK, lambda k: x0(group, k).wait_send())
        each(1, 4, lambda j: a1(group, j).wait_send())
        each(1, CHIPS, lambda j: b1(group, j, 0).wait_send())
    each(1, HEAD, lambda j: b2(j).wait_send())
    for p in range(2):
        each(1 - p, CHIPS, lambda j: a2(0, p, j, y_lo, chip).wait_send())
    rs3.wait_send()


def per_device(hidden_rows, head_weight, teacher_logits):
    hbm = pl.BlockSpec(memory_space=pltpu.MemorySpace.HBM)
    vmem = pl.BlockSpec(memory_space=pltpu.VMEM)
    dma = pltpu.SemaphoreType.DMA
    weight_grad, input_grad = pl.pallas_call(
        kernel,
        out_shape=(
            pltpu.VMEM((D, COLS), BF16),
            jax.ShapeDtypeStruct((TOK // (HEAD * VOC), D), F32),
        ),
        in_specs=[hbm, hbm, hbm],
        out_specs=(vmem, vmem),
        scratch_shapes=[
            pltpu.VMEM((TOK // (HEAD * VOC), D), BF16),
            pltpu.VMEM((D, COLS), BF16),
            pltpu.VMEM((ROWS, COLS * VOC), BF16),
            pltpu.VMEM((TOK, COLS), BF16),
            pltpu.VMEM((16, CW), F32),
            pltpu.VMEM((2, 16, CW), BF16),
            pltpu.VMEM((2 * VOC, 16, CW), BF16),
            pltpu.VMEM((HR, HALF), F32),
            pltpu.VMEM((2, TOK, HALF), BF16),
            pltpu.VMEM((D, TOK), BF16),
            pltpu.VMEM((NB, TOK, BW), F32),
            pltpu.VMEM((TOK, COLS), BF16),
            pltpu.VMEM((2, GR, 128), F32),
            pltpu.VMEM((2, TOK, 128), F32),
            pltpu.VMEM((8, 128), F32),
            pltpu.VMEM((VOC, 8, 128), F32),
            pltpu.VMEM((2, 8, 128), F32),
            pltpu.VMEM((2, VOC, 8, 128), F32),
            pltpu.VMEM((2 * DK, GR, BW), BF16),
            pltpu.VMEM((2 * DK, GR, BW), BF16),
            pltpu.VMEM((2, 4, HR, BW), BF16),
            pltpu.VMEM((2, 4, HR, BW), BF16),
            pltpu.VMEM((2, CHIPS, 8, BW), F32),
            pltpu.VMEM((2, CHIPS, 8, BW), F32),
            pltpu.VMEM((2, CHIPS, 32, BW), BF16),
            pltpu.VMEM((2, CHIPS, 32, BW), BF16),
            pltpu.VMEM((HEAD, 8, BW), F32),
            pltpu.VMEM((HEAD, 8, BW), F32),
            pltpu.VMEM((8, HALF), F32),
            pltpu.VMEM((8, HALF), F32),
            dma((4,)),
            dma((2 * VOC,)), dma((2 * VOC,)), dma((VOC,)), dma((VOC,)), dma((VOC,)), dma((VOC,)),
            dma((8,)), dma((8,)), dma((8,)), dma((8,)),
            dma((2 * VOC,)), dma((2 * VOC,)), dma((2 * DK,)), dma((2 * DK,)),
            dma((8,)), dma((8,)), dma((2 * CHIPS,)), dma((2 * CHIPS,)),
            dma((2 * CHIPS,)), dma((2 * CHIPS,)), dma((HEAD,)), dma((HEAD,)), dma, dma,
        ],
        compiler_params=pltpu.CompilerParams(
            collective_id=0, has_side_effects=True, vmem_limit_bytes=44 * 1024 * 1024
        ),
        cost_estimate=pl.CostEstimate(
            flops=6 * TOK * D * COLS, bytes_accessed=20 * 1024 * 1024, transcendentals=3 * TOK * COLS
        ),
    )(hidden_rows, head_weight[0], teacher_logits[0])
    return weight_grad[None], input_grad


def solution(mesh):
    return jax.shard_map(
        per_device,
        mesh=mesh,
        in_specs=(P(("head", "vocab"), None), P("head", None, "vocab"), P("head", "vocab", None)),
        out_specs=(P("head", None, "vocab"), P(("head", "vocab"), None)),
        check_vma=False,
    )
```
